256 devices in a mesh: enc: 32 (over z, x), tp: 8 (over y, core), rep: 1.
Axes of the slice: x: 4, y: 4, z: 8, core: 2. Of those that a mesh axis runs over, the one named last changes fastest.
Arguments:
- patches: bfloat16 [128, 64, 5120], P(('rep', 'enc')), may hold values from -6 to 6
- slot_page: int32 [128], P('rep'), may hold values from -1 to 63, as said below
- page_start: int32 [64], P('rep'), may hold values from 0 to 8128, as said below
- patch_gain: float32 [1280], replicated, may hold values from 0.25 to 1.75
- patch_bias: float32 [1280], replicated, may hold values from -3 to 3
- merge_in: bfloat16 [5120, 5120], P(None, 'tp'), may hold values from -0.078125 to 0.078125
- merge_out: bfloat16 [5120, 8192], P('tp', 'enc'), may hold values from -0.078125 to 0.078125
- text: bfloat16 [8192, 8192], P(('rep', 'enc'), 'tp'), may hold values from -6 to 6
- norm_gain: float32 [8192], P('tp'), may hold values from 0.25 to 1.75
- kv_weight: bfloat16 [8192, 2048], P('tp', 'enc'), may hold values from -0.0625 to 0.0625
Outputs:
- keys_out: bfloat16 [8192, 1024], P(('rep', 'enc'), 'tp')
- values_out: bfloat16 [8192, 1024], P(('rep', 'enc'), 'tp')
The draws below stay inside these ranges and needn't reach their ends.
Inputs may be any that keep to these rules, and one draw needn't show every extreme that they name: `slot_page`: every page 0 to 63 is held in exactly one slot; slots i * 4 to (i + 1) * 4 - 1 form device i of enc, and the most live pages of one device is exactly 4. `page_start`: page k lies whole inside the block of 256 tokens number k // 2; pages do not intersect.
All inputs are finite; a program needn't handle non-finite values.
Results may differ from the reference program's by a relative error of at most 0.024.
Values may be sent and summed in bfloat16 or wider, within the bound.
No kernel may reach another device: no remote copies, remote signals or barrier semaphores. Data moves between devices by JAX's collectives and lax.ppermute only.
A program may use at most 128 MiB of HBM per device.

```python
import jax
import jax.numpy as jnp
from jax import lax

D = 8192
KV_HEADS = 8
HEAD = 128
PATCH_W = 1280
PF = 5120
PAGE_ROWS = 64
SPAN_DEV = 256
SLOTS = 4
PG_SH = 2
PAGES = 64
SLOT_ALL = 128
SPAN = 8192
N_ENC = 32
N_TP = 8


def draw_slot_page(key, part):
    key = jax.random.fold_in(key, 11)
    key_heavy, key_score, key_order = jax.random.split(key, 3)
    heavy = jax.random.randint(key_heavy, (), 0, N_ENC)
    slot_index = jnp.arange(SLOT_ALL, dtype=jnp.int32)
    device = slot_index // SLOTS
    scores = jax.random.randint(key_score, (SLOT_ALL,), 0, 1 << 16) * SLOT_ALL + slot_index
    scores = jnp.where(device == heavy, slot_index - SLOT_ALL, scores)
    ranking = jnp.argsort(jnp.argsort(scores)).astype(jnp.int32)
    page_order = jax.random.permutation(key_order, PAGES).astype(jnp.int32)
    picked = page_order[jnp.clip(ranking, 0, PAGES - 1)]
    return jnp.where(ranking < PAGES, picked, -1).astype(jnp.int32)


def draw_page_start(key, part):
    key = jax.random.fold_in(key, 23)
    spare_rows = SPAN_DEV - PG_SH * PAGE_ROWS
    remaining = jnp.full((N_ENC,), spare_rows, dtype=jnp.int32)
    offset = jnp.zeros((N_ENC,), dtype=jnp.int32)
    base_rows = jnp.arange(N_ENC, dtype=jnp.int32) * SPAN_DEV
    starts = []
    for index in range(PG_SH):
        key, sub_key = jax.random.split(key)
        gap_rows = jnp.minimum(jax.random.randint(sub_key, (N_ENC,), 0, spare_rows + 1), remaining)
        offset = offset + gap_rows
        starts.append(base_rows + offset)
        offset = offset + PAGE_ROWS
        remaining = remaining - gap_rows
    return jnp.stack(starts, axis=1).reshape(PAGES).astype(jnp.int32)


def steps_of(own_key, dims, cuts, least, high):
    def one(axis_at, blocks):
        steps = jax.random.uniform(jax.random.fold_in(jax.random.fold_in(own_key, 6), axis_at), (blocks,), jnp.float32, least / len(cuts), high / len(cuts))
        return jnp.repeat(jnp.exp(steps), dims[axis_at] // blocks).reshape((-1,) + (1,) * (len(dims) - axis_at - 1))

    factor_of = one(*cuts[0])
    for cut in cuts[1:]:
        factor_of = factor_of * one(*cut)
    return factor_of


def normal_values(stream_key, dims, scale, reach, shards=(), kind=jnp.bfloat16):
    factor_of = steps_of(stream_key, dims, shards, -0.22, 0.18) if shards else 1.0
    drawn = jax.random.normal(stream_key, dims, jnp.float32) * scale * factor_of
    return jnp.minimum(jnp.maximum(drawn, -reach), reach).astype(kind)


def setup_inputs(seed: int = 0, part: int = 0) -> dict:
    key_of = jax.random.split(jax.random.key(seed), 11)
    part_keys = jax.random.split(jax.random.fold_in(key_of[10], part), 11)
    return {
        "patches": normal_values(part_keys[0], (SLOT_ALL, PAGE_ROWS, PF), 1.0, 6.0, ((0, 32),)),
        "slot_page": draw_slot_page(jax.random.fold_in(jax.random.fold_in(key_of[10], part), 71), part),
        "page_start": draw_page_start(jax.random.fold_in(jax.random.fold_in(key_of[10], part), 71), part),
        "patch_gain": jnp.clip(1.0 + 0.15 * jax.random.normal(key_of[3], (PATCH_W,), jnp.float32), 0.25, 1.75),
        "patch_bias": normal_values(key_of[4], (PATCH_W,), 0.5, 3.0, (), jnp.float32),
        "merge_in": normal_values(key_of[5], (PF, PF), PF ** -0.5, 0.078125, ((1, 8),)),
        "merge_out": normal_values(key_of[6], (PF, D), PF ** -0.5, 0.078125, ((0, 8), (1, 32))),
        "text": normal_values(part_keys[7], (SPAN, D), 1.0, 6.0, ((0, 32), (1, 8))),
        "norm_gain": jnp.clip(1.0 + 0.15 * jax.random.normal(key_of[8], (D,), jnp.float32), 0.25, 1.75),
        "kv_weight": normal_values(key_of[9], (D, 2 * KV_HEADS * HEAD), D ** -0.5, 0.0625, ((0, 8), (1, 32))),
    }


EPS = 1e-06
THETA = 1000000.0

def patch_norm(flat_rows, patch_gain, patch_bias):
    shaped = flat_rows.astype(jnp.float32).reshape(flat_rows.shape[0], -1, patch_gain.shape[0])
    center = lax.optimization_barrier(jnp.mean(shaped, axis=-1, keepdims=True))
    spread = lax.optimization_barrier(jnp.mean(jnp.square(shaped - center), axis=-1, keepdims=True))
    normed = (shaped - center) * lax.rsqrt(spread + EPS) * patch_gain + patch_bias
    return normed.reshape(flat_rows.shape).astype(jnp.bfloat16)

def rotate_keys(key_heads, positions):
    half_size = key_heads.shape[-1] // 2
    frequency = THETA ** (-jnp.arange(half_size, dtype=jnp.float32) * 2.0 / key_heads.shape[-1])
    angles = positions[:, None, None] * frequency
    lower_half = key_heads[..., :half_size]
    upper_half = key_heads[..., half_size:]
    return jnp.concatenate([lower_half * jnp.cos(angles) - upper_half * jnp.sin(angles), upper_half * jnp.cos(angles) + lower_half * jnp.sin(angles)], axis=-1)

def grouped_product(left, right, groups):
    width = left.shape[1] // groups
    total = jnp.zeros((left.shape[0], right.shape[1]), jnp.float32)
    for group in range(groups):
        part = jnp.dot(left[:, group * width:(group + 1) * width], right[group * width:(group + 1) * width], preferred_element_type=jnp.float32).astype(jnp.bfloat16)
        part = lax.optimization_barrier(part)
        total = total + part.astype(jnp.float32)
    return total

def reference(patches, slot_page, page_start, patch_gain, patch_bias, merge_in, merge_out, text, norm_gain, kv_weight):
    flat_rows = patch_norm(patches.reshape(SLOT_ALL * PAGE_ROWS, PF), patch_gain, patch_bias)
    hidden = jax.nn.gelu(jnp.dot(flat_rows, merge_in, preferred_element_type=jnp.float32), approximate=False).astype(jnp.bfloat16)
    merged = grouped_product(hidden, merge_out, N_TP).astype(jnp.bfloat16)
    merged = merged.reshape(SLOT_ALL, PAGE_ROWS * D)
    chooser = (slot_page[None, :] == jnp.arange(PAGES, dtype=jnp.int32)[:, None]).astype(jnp.bfloat16)
    visual = jnp.dot(chooser, merged, preferred_element_type=jnp.float32).astype(jnp.bfloat16)
    visual = visual.reshape(PAGES * PAGE_ROWS, D)
    row_index = (page_start[:, None] + jnp.arange(PAGE_ROWS, dtype=jnp.int32)[None, :]).reshape(-1)
    assembled = text.at[row_index].set(visual)
    mean_square = lax.optimization_barrier(jnp.mean(jnp.square(assembled.astype(jnp.float32)), axis=1))
    normed = (assembled.astype(jnp.float32) * lax.rsqrt(mean_square + EPS)[:, None] * norm_gain).astype(jnp.bfloat16)
    kv_all = grouped_product(normed, kv_weight, N_TP).reshape(SPAN, KV_HEADS, 2, HEAD)
    rotated = rotate_keys(kv_all[:, :, 0], jnp.arange(SPAN).astype(jnp.float32))
    keys_out = rotated.reshape(SPAN, KV_HEADS * HEAD).astype(jnp.bfloat16)
    values_out = kv_all[:, :, 1].reshape(SPAN, KV_HEADS * HEAD).astype(jnp.bfloat16)
    return (keys_out, values_out)
```

```python
import functools

import jax
import jax.numpy as jnp
from jax import lax
from jax.experimental import pallas as pl
from jax.experimental.pallas import tpu as pltpu
from jax.sharding import PartitionSpec as P

EPS = 1e-06
THETA = 1000000.0
NZ, NX, NY, NC = 8, 4, 4, 2
VMEM_LIMIT = 40 * 1024 * 1024
BF = jnp.bfloat16
F32 = jnp.float32

GROUPS_Z = [[z * NX + x for z in range(NZ)] for x in range(NX)]


def shift_x(d):
    return [(z * NX + x, z * NX + (x + d) % NX) for z in range(NZ) for x in range(NX)]


def shift_y(d):
    return [(y * NC + c, (y + d) % NY * NC + c) for y in range(NY) for c in range(NC)]


SWAP_CORE = [(t, t ^ 1) for t in range(NY * NC)]


def hidden_kernel(slots, patch_ref, gain_ref, bias_ref, weight_ref, out_ref, acc_ref):
    step = pl.program_id(0)
    part = patch_ref[...].astype(F32)
    center = jnp.mean(part, axis=-1, keepdims=True)
    part = part - center
    spread = jnp.mean(part * part, axis=-1, keepdims=True)
    normed = part * lax.rsqrt(spread + EPS) * gain_ref[...] + bias_ref[...]
    term = jnp.dot(normed.astype(BF), weight_ref[...], preferred_element_type=F32)

    @pl.when(step == 0)
    def _():
        acc_ref[...] = term

    @pl.when(step > 0)
    def _():
        acc_ref[...] += term

    @pl.when(step == pl.num_programs(0) - 1)
    def _():
        total = acc_ref[...]
        total = 0.5 * total * (1.0 + lax.erf(total * 0.7071067811865476))
        rows = total.shape[0] // slots
        chunk = rows // NZ
        pieces = [
            total[slot * rows + z * chunk : slot * rows + (z + 1) * chunk]
            for z in range(NZ)
            for slot in range(slots)
        ]
        out_ref[...] = jnp.concatenate(pieces, axis=0).astype(BF)


def hidden_rows(patches, patch_gain, patch_bias, merge_in):
    slots, rows, feature = patches.shape
    width = patch_gain.shape[0]
    flat = patches.reshape(slots * rows, feature)
    out_width = merge_in.shape[1]
    return pl.pallas_call(
        functools.partial(hidden_kernel, slots),
        grid=(feature // width,),
        in_specs=[
            pl.BlockSpec((slots * rows, width), lambda i: (0, i)),
            pl.BlockSpec((1, width), lambda i: (0, 0)),
            pl.BlockSpec((1, width), lambda i: (0, 0)),
            pl.BlockSpec((width, out_width), lambda i: (i, 0)),
        ],
        out_specs=pl.BlockSpec((slots * rows, out_width), lambda i: (0, 0)),
        out_shape=jax.ShapeDtypeStruct((slots * rows, out_width), BF),
        scratch_shapes=[pltpu.VMEM((slots * rows, out_width), F32)],
        compiler_params=pltpu.CompilerParams(vmem_limit_bytes=VMEM_LIMIT),
        cost_estimate=pl.CostEstimate(
            flops=2 * slots * rows * feature * out_width,
            bytes_accessed=2 * feature * (out_width + slots * rows),
            transcendentals=0,
        ),
    )(flat, patch_gain[None], patch_bias[None], merge_in)


def send_kernel(order_ref, target_ref, a, b, c, d, weight_ref, live_ref, out_ref):
    step = pl.program_id(0)

    @pl.when(step == 0)
    def _():
        target = target_ref[...]
        total = None
        for index, piece in enumerate((a, b, c, d)):
            rows = piece.shape[0]
            place = lax.broadcasted_iota(jnp.int32, (target.shape[0], rows), 1) + index * rows
            pick = jnp.where(place == target, 1.0, 0.0).astype(BF)
            term = jnp.dot(pick, piece[...], preferred_element_type=F32)
            total = term if total is None else total + term
        live_ref[...] = total.astype(BF)

    out_ref[0] = jnp.dot(live_ref[...], weight_ref[0], preferred_element_type=F32).astype(BF)


def send_parts(order, target, pieces, weights):
    rows, depth = target.shape[0], pieces[0].shape[1]
    width = weights.shape[2]
    whole = pl.BlockSpec(pieces[0].shape, lambda i, order: (0, 0))
    return pl.pallas_call(
        send_kernel,
        grid_spec=pltpu.PrefetchScalarGridSpec(
            num_scalar_prefetch=1,
            grid=(NY,),
            in_specs=[pl.BlockSpec((rows, 1), lambda i, order: (0, 0))]
            + [whole] * 4
            + [pl.BlockSpec((1, depth, width), lambda i, order: (order[i], 0, 0))],
            out_specs=[
                pl.BlockSpec((rows, depth), lambda i, order: (0, 0)),
                pl.BlockSpec((1, rows, width), lambda i, order: (i, 0, 0)),
            ],
        ),
        out_shape=[
            jax.ShapeDtypeStruct((rows, depth), BF),
            jax.ShapeDtypeStruct((NY, rows, width), BF),
        ],
        compiler_params=pltpu.CompilerParams(vmem_limit_bytes=VMEM_LIMIT),
        cost_estimate=pl.CostEstimate(
            flops=2 * rows * depth * (width * NY + 2 * rows),
            bytes_accessed=2 * (depth * width * NY + rows * width * NY),
            transcendentals=0,
        ),
    )(order, target, *pieces, weights)


def keep_kernel(order_ref, live_ref, weight_ref, got_ref, *out_refs):
    step = pl.program_id(0)
    own = jnp.dot(live_ref[...], weight_ref[0], preferred_element_type=F32).astype(BF)
    total = (own.astype(F32) + got_ref[0].astype(F32)).astype(BF)
    for index, out_ref in enumerate(out_refs):

        @pl.when(step == index)
        def _(out_ref=out_ref):
            out_ref[...] = total


def keep_parts(order, live, weights, got):
    rows, depth = live.shape
    width = weights.shape[2]
    return pl.pallas_call(
        keep_kernel,
        grid_spec=pltpu.PrefetchScalarGridSpec(
            num_scalar_prefetch=1,
            grid=(NY,),
            in_specs=[
                pl.BlockSpec((rows, depth), lambda i, order: (0, 0)),
                pl.BlockSpec((1, depth, width), lambda i, order: (order[i], 0, 0)),
                pl.BlockSpec((1, rows, width), lambda i, order: (i, 0, 0)),
            ],
            out_specs=[pl.BlockSpec((rows, width), lambda i, order: (0, 0))] * NY,
        ),
        out_shape=[jax.ShapeDtypeStruct((rows, width), BF)] * NY,
        compiler_params=pltpu.CompilerParams(vmem_limit_bytes=VMEM_LIMIT),
        cost_estimate=pl.CostEstimate(
            flops=2 * rows * depth * width * NY,
            bytes_accessed=2 * (depth * width * NY + 2 * rows * width * NY),
            transcendentals=0,
        ),
    )(order, live, weights, got)


def project_kernel(target_ref, moved_ref, text_ref, weight_ref, out_ref, rows_ref, squares_ref):
    step = pl.program_id(0)
    span = text_ref.shape[0]

    @pl.when(step == 0)
    def _():
        target = target_ref[...]
        place = lax.broadcasted_iota(jnp.int32, (span, target.shape[1]), 0) == target
        pick = jnp.where(place, 1.0, 0.0)
        covered = jnp.sum(pick, axis=1, keepdims=True) > 0.5
        pick = pick.astype(BF)
        width = moved_ref.shape[2]
        ones = jnp.ones((16, width), BF)
        contract = (((1,), (1,)), ((), ()))
        squares = jnp.zeros((16, span), F32)
        for x in range(NX):
            stacked = jnp.concatenate([moved_ref[z * NX + x] for z in range(NZ)], axis=0)
            put = jnp.dot(pick, stacked, preferred_element_type=F32)
            columns = slice(x * width, (x + 1) * width)
            mixed = jnp.where(covered, put, text_ref[:, columns].astype(F32))
            rows_ref[:, columns] = mixed.astype(BF)
            square = mixed * mixed
            high = square.astype(BF)
            low = (square - high.astype(F32)).astype(BF)
            for term in (high, low):
                squares += lax.dot_general(ones, term, contract, preferred_element_type=F32)
        high = squares.astype(BF).astype(F32)
        line = lax.broadcasted_iota(jnp.int32, squares.shape, 0)
        squares_ref[...] = jnp.where(
            line == 0, high, jnp.where(line == 1, squares - high, 0.0)
        ).astype(BF)

    out_ref[0, :span] = jnp.dot(
        rows_ref[...], weight_ref[0], preferred_element_type=F32
    ).astype(BF)
    out_ref[0, span:] = squares_ref[...]


def project(target, moved, text, weights):
    span, features = text.shape
    heads, _, width = weights.shape
    return pl.pallas_call(
        project_kernel,
        grid=(heads,),
        in_specs=[
            pl.BlockSpec(target.shape, lambda i: (0, 0)),
            pl.BlockSpec(moved.shape, lambda i: (0, 0, 0)),
            pl.BlockSpec(text.shape, lambda i: (0, 0)),
            pl.BlockSpec((1, features, width), lambda i: (i, 0, 0)),
        ],
        out_specs=pl.BlockSpec((1, span + 16, width), lambda i: (i, 0, 0)),
        out_shape=jax.ShapeDtypeStruct((heads, span + 16, width), BF),
        scratch_shapes=[pltpu.VMEM((span, features), BF), pltpu.VMEM((16, span), BF)],
        compiler_params=pltpu.CompilerParams(vmem_limit_bytes=VMEM_LIMIT),
        cost_estimate=pl.CostEstimate(
            flops=2 * span * features * (width * heads + 2 * span),
            bytes_accessed=2 * heads * width * (features + span),
            transcendentals=0,
        ),
    )(target, moved, text, weights)


def finish_kernel(features, parts_ref, cos_ref, sin_ref, keys_ref, values_ref):
    span = keys_ref.shape[0]
    head = keys_ref.shape[1]
    total = parts_ref[0].astype(F32)
    for index in range(1, parts_ref.shape[0]):
        total = total + parts_ref[index].astype(F32)
    squares = total[span : span + 1] + total[span + 1 : span + 2]
    diagonal = lax.broadcasted_iota(jnp.int32, (span, span), 0) == lax.broadcasted_iota(
        jnp.int32, (span, span), 1
    )
    squares = jnp.sum(jnp.where(diagonal, squares, 0.0), axis=1, keepdims=True)
    scale = lax.rsqrt(squares / features + EPS)
    key = total[:span, :head] * scale
    turned = pltpu.roll(key, head // 2, 1)
    keys_ref[...] = (key * cos_ref[...] + turned * sin_ref[...]).astype(BF)
    values_ref[...] = (total[:span, head:] * scale).astype(BF)


def finish(features, parts, cos, sin):
    span, head = cos.shape
    return pl.pallas_call(
        functools.partial(finish_kernel, features),
        out_shape=[jax.ShapeDtypeStruct((span, head), BF)] * 2,
        compiler_params=pltpu.CompilerParams(vmem_limit_bytes=VMEM_LIMIT),
    )(parts, cos, sin)


def rotary(positions, head):
    half = head // 2
    frequency = THETA ** (-jnp.arange(half, dtype=F32) * 2.0 / head)
    angles = positions[:, None] * frequency
    cos, sin = jnp.cos(angles), jnp.sin(angles)
    return jnp.concatenate([cos, cos], axis=1), jnp.concatenate([-sin, sin], axis=1)


def body(
    patches,
    slot_page,
    page_start,
    patch_gain,
    patch_bias,
    merge_in,
    merge_out,
    text,
    norm_gain,
    kv_weight,
):
    enc_index, tp_index = lax.axis_index("enc"), lax.axis_index("tp")
    x_index = enc_index % NX
    y_index, core = tp_index // NC, tp_index % NC
    slots, page_rows, _ = patches.shape
    pages = page_start.shape[0]
    span, features = text.shape
    chunk = page_rows // NZ
    half = features // 2

    weights = lax.all_gather(merge_out, "enc", axis_index_groups=GROUPS_Z)

    scaled = (kv_weight.astype(F32) * norm_gain[:, None]).astype(BF)
    packed = jnp.concatenate([scaled[:half], scaled[half:]], axis=1)
    quarter = kv_weight.shape[1]
    by_shift = [packed] + [lax.ppermute(packed, "enc", shift_x(d)) for d in range(1, NX)]
    by_x = jnp.stack(by_shift)[(x_index - jnp.arange(NX)) % NX]
    head_weight = by_x.reshape(NX, half, 2, quarter).transpose(2, 1, 0, 3)
    head_weight = head_weight.reshape(features, NX * quarter)
    kv_all = lax.all_gather(head_weight, "enc", axis_index_groups=GROUPS_Z)

    hidden = hidden_rows(patches, patch_gain, patch_bias, merge_in)
    dealt = lax.all_to_all(hidden, "enc", 0, 0, axis_index_groups=GROUPS_Z, tiled=True)
    pieces = [dealt] + [lax.ppermute(dealt, "enc", shift_x(d)) for d in range(1, NX)]

    page_ids = jnp.arange(pages, dtype=jnp.int32)
    slot_ids = jnp.arange(slot_page.shape[0], dtype=jnp.int32)
    slot_of = jnp.sum(
        jnp.where(slot_page[None, :] == page_ids[:, None], slot_ids[None, :], 0), axis=1
    )
    holder = slot_of // slots
    place = (x_index - holder % NX) % NX * NZ + holder // NX
    place = (place * slots + slot_of % slots) * chunk
    target = (place[:, None] + jnp.arange(chunk, dtype=jnp.int32)[None, :]).reshape(-1, 1)

    shifted = (y_index + jnp.arange(NY, dtype=jnp.int32)) % NY * NC
    live, away = send_parts(shifted + (1 - core), target, pieces, weights)
    got = lax.ppermute(away, "tp", SWAP_CORE)
    parts = keep_parts(shifted + core, live, weights, got)
    total = parts[0].astype(F32)
    for d in range(1, NY):
        total = total + lax.ppermute(parts[d], "tp", shift_y(d)).astype(F32)
    merged = total.astype(BF)

    moved = lax.all_to_all(merged, "enc", 0, 0, tiled=True)
    per_block = pages // (NZ * NX)
    moved = moved.reshape(NZ * NX, per_block * chunk, merged.shape[1])
    starts = lax.dynamic_slice_in_dim(page_start, enc_index * per_block, per_block)
    starts = starts - enc_index * span
    rows = (
        jnp.arange(NZ, dtype=jnp.int32)[:, None, None] * chunk
        + starts[None, :, None]
        + jnp.arange(chunk, dtype=jnp.int32)[None, None, :]
    ).reshape(1, -1)
    kv_parts = project(rows, moved, text, kv_all)

    sent = kv_parts.reshape(-1, kv_parts.shape[2])
    gathered = lax.all_to_all(sent, "tp", 0, 0, tiled=True).reshape(kv_parts.shape)
    positions = (enc_index * span + jnp.arange(span, dtype=jnp.int32)).astype(F32)
    cos, sin = rotary(positions, kv_parts.shape[2] // 2)
    return tuple(finish(features * NY * NC, gathered, cos, sin))


def solution(mesh):
    return jax.shard_map(
        body,
        mesh=mesh,
        in_specs=(
            P(("rep", "enc"), None, None),
            P("rep"),
            P("rep"),
            P(),
            P(),
            P(None, "tp"),
            P("tp", "enc"),
            P(("rep", "enc"), "tp"),
            P("tp"),
            P("tp", "enc"),
        ),
        out_specs=(P(("rep", "enc"), "tp"), P(("rep", "enc"), "tp")),
        check_vma=False,
    )
```

```python
import functools

import jax
import jax.numpy as jnp
from jax import lax
from jax.experimental import pallas as pl
from jax.experimental.pallas import tpu as pltpu
from jax.sharding import PartitionSpec as P

EPS = 1e-06
THETA = 1000000.0
NZ, NX, NY, NC = 8, 4, 4, 2
TAILS = 2
VMEM_LIMIT = 24 * 1024 * 1024
BF = jnp.bfloat16
F32 = jnp.float32

GROUPS_Z = [[z * NX + x for z in range(NZ)] for x in range(NX)]


def shift_x(d):
    return [(z * NX + x, z * NX + (x + d) % NX) for z in range(NZ) for x in range(NX)]


def shift_y(d):
    return [(y * NC + c, (y + d) % NY * NC + c) for y in range(NY) for c in range(NC)]


SWAP_CORE = [(t, t ^ 1) for t in range(NY * NC)]


IN_VMEM = pl.BlockSpec(memory_space=pltpu.VMEM)
IN_SMEM = pl.BlockSpec(memory_space=pltpu.SMEM)
IN_HBM = pl.BlockSpec(memory_space=pltpu.HBM)


def in_hbm(array):
    return pltpu.with_memory_space_constraint(array, pltpu.HBM)


def hidden_kernel(
    slots, patch_ref, gain_ref, bias_ref, weight_ref, out_ref, patch_buf, weight_buf, sems
):
    width = weight_buf.shape[1]
    copies = []
    for i in range(weight_buf.shape[0]):
        part = pl.ds(i * width, width)
        pair = (
            pltpu.make_async_copy(patch_ref.at[:, part], patch_buf.at[i], sems.at[0, i]),
            pltpu.make_async_copy(weight_ref.at[part], weight_buf.at[i], sems.at[1, i]),
        )
        for copy in pair:
            copy.start()
        copies.append(pair)
    gain, bias = gain_ref[...][None, :], bias_ref[...][None, :]
    total = None
    for i, pair in enumerate(copies):
        pair[0].wait()
        part = patch_buf[i].astype(F32)
        center = jnp.mean(part, axis=-1, keepdims=True)
        part = part - center
        spread = jnp.mean(part * part, axis=-1, keepdims=True)
        normed = (part * lax.rsqrt(spread + EPS) * gain + bias).astype(BF)
        pair[1].wait()
        term = jnp.dot(normed, weight_buf[i], preferred_element_type=F32)
        total = term if total is None else total + term
    total = 0.5 * total * (1.0 + lax.erf(total * 0.7071067811865476))
    rows = total.shape[0] // slots
    chunk = rows // NZ
    pieces = [
        total[slot * rows + z * chunk : slot * rows + (z + 1) * chunk]
        for z in range(NZ)
        for slot in range(slots)
    ]
    out_ref[...] = jnp.concatenate(pieces, axis=0).astype(BF)


def hidden_rows(patches, patch_gain, patch_bias, merge_in):
    slots, rows, feature = patches.shape
    width = patch_gain.shape[0]
    groups = feature // width
    flat = patches.reshape(slots * rows, feature)
    out_width = merge_in.shape[1]
    return pl.pallas_call(
        functools.partial(hidden_kernel, slots),
        in_specs=[
            pl.BlockSpec(memory_space=pltpu.HBM),
            pl.BlockSpec(memory_space=pltpu.VMEM),
            pl.BlockSpec(memory_space=pltpu.VMEM),
            pl.BlockSpec(memory_space=pltpu.HBM),
        ],
        out_specs=pl.BlockSpec(memory_space=pltpu.VMEM),
        out_shape=jax.ShapeDtypeStruct((slots * rows, out_width), BF),
        scratch_shapes=[
            pltpu.VMEM((groups, slots * rows, width), BF),
            pltpu.VMEM((groups, width, out_width), BF),
            pltpu.SemaphoreType.DMA((2, groups)),
        ],
        compiler_params=pltpu.CompilerParams(vmem_limit_bytes=VMEM_LIMIT),
        cost_estimate=pl.CostEstimate(
            flops=2 * slots * rows * feature * out_width,
            bytes_accessed=2 * feature * (out_width + slots * rows),
            transcendentals=0,
        ),
    )(in_hbm(flat), patch_gain, patch_bias, in_hbm(merge_in))


def fetch(order_ref, weight_ref, buf, sems):
    copies = [
        pltpu.make_async_copy(
            weight_ref.at[order_ref[i], : buf.shape[1]], buf.at[i], sems.at[i]
        )
        for i in range(buf.shape[0])
    ]
    for copy in copies:
        copy.start()
    return copies


def send_kernel(order_ref, target_ref, a, b, c, d, weight_ref, live_ref, out_ref, buf, sems):
    copies = fetch(order_ref, weight_ref, buf, sems)
    target = target_ref[...]
    total = None
    for index, piece in enumerate((a, b, c, d)):
        rows = piece.shape[0]
        place = lax.broadcasted_iota(jnp.int32, (target.shape[0], rows), 1) + index * rows
        pick = jnp.where(place == target, 1.0, 0.0).astype(BF)
        term = jnp.dot(pick, piece[...], preferred_element_type=F32)
        total = term if total is None else total + term
    live_ref[...] = total.astype(BF)
    for i, copy in enumerate(copies):
        copy.wait()
        out_ref[i] = jnp.dot(live_ref[...], buf[i], preferred_element_type=F32).astype(BF)


def send_parts(order, target, pieces, weights):
    rows, depth = target.shape[0], pieces[0].shape[1]
    width = weights.shape[2]
    return pl.pallas_call(
        send_kernel,
        in_specs=[IN_SMEM, IN_VMEM] + [IN_VMEM] * 4 + [IN_HBM],
        out_specs=[IN_VMEM, IN_VMEM],
        out_shape=[
            jax.ShapeDtypeStruct((rows, depth), BF),
            jax.ShapeDtypeStruct((NY, rows, width), BF),
        ],
        scratch_shapes=[pltpu.VMEM((NY, depth, width), BF), pltpu.SemaphoreType.DMA((NY,))],
        compiler_params=pltpu.CompilerParams(vmem_limit_bytes=VMEM_LIMIT),
        cost_estimate=pl.CostEstimate(
            flops=2 * rows * depth * (width * NY + 2 * rows),
            bytes_accessed=2 * (depth * width * NY + rows * width * NY),
            transcendentals=0,
        ),
    )(order, target, *pieces, in_hbm(weights))


def keep_kernel(order_ref, live_ref, weight_ref, got_ref, a, b, c, d, buf, sems):
    copies = fetch(order_ref, weight_ref, buf, sems)
    for i, out_ref in enumerate((a, b, c, d)):
        copies[i].wait()
        own = jnp.dot(live_ref[...], buf[i], preferred_element_type=F32).astype(BF)
        out_ref[...] = (own.astype(F32) + got_ref[i].astype(F32)).astype(BF)


def keep_parts(order, live, weights, got):
    rows, depth = live.shape
    width = weights.shape[2]
    return pl.pallas_call(
        keep_kernel,
        in_specs=[IN_SMEM, IN_VMEM, IN_HBM, IN_VMEM],
        out_specs=[IN_VMEM] * NY,
        out_shape=[jax.ShapeDtypeStruct((rows, width), BF)] * NY,
        scratch_shapes=[pltpu.VMEM((NY, depth, width), BF), pltpu.SemaphoreType.DMA((NY,))],
        compiler_params=pltpu.CompilerParams(vmem_limit_bytes=VMEM_LIMIT),
        cost_estimate=pl.CostEstimate(
            flops=2 * rows * depth * width * NY,
            bytes_accessed=2 * (depth * width * NY + 2 * rows * width * NY),
            transcendentals=0,
        ),
    )(order, live, in_hbm(weights), got)


def put_head(i, order_ref, rows_ref, first_ref, rest_refs, out_ref, more=None):
    head = order_ref[i]
    rows = first_ref.shape[1] // NX
    lines = []
    for d in range(NX):
        line = [first_ref[i, d * rows : (d + 1) * rows]]
        line += [ref[head] for ref in rest_refs[d * TAILS : (d + 1) * TAILS]]
        lines.append(jnp.concatenate(line, axis=1))
    part = jnp.dot(
        jnp.concatenate(lines, axis=0), rows_ref[...], preferred_element_type=F32
    ).astype(BF)
    for d in range(NX):
        place = pl.ds(pl.multiple_of(order_ref[NY + d] * rows, rows), rows)
        piece = part[d * rows : (d + 1) * rows]
        if more is not None:
            piece = (piece.astype(F32) + more[i, place].astype(F32)).astype(BF)
        out_ref[place] = piece


def two_lines(squares):
    squares = jnp.broadcast_to(squares, (16, squares.shape[1]))
    high = squares.astype(BF).astype(F32)
    line = lax.broadcasted_iota(jnp.int32, squares.shape, 0)
    return jnp.where(line == 0, high, jnp.where(line == 1, squares - high, 0.0)).astype(BF)


def project_send_kernel(order_ref, target_ref, moved_ref, text_ref, first_ref, *refs):
    rest_refs, (rows_ref, squares_ref, out_ref, buf, sems) = refs[:-5], refs[-5:]
    copies = fetch(order_ref, first_ref, buf, sems)
    span = text_ref.shape[0]
    target = target_ref[...]
    place = lax.broadcasted_iota(jnp.int32, (span, target.shape[1]), 0) == target
    pick = jnp.where(place, 1.0, 0.0)
    covered = jnp.sum(pick, axis=1, keepdims=True) > 0.5
    pick = pick.astype(BF)
    width = moved_ref.shape[2]
    squares = jnp.zeros((1, span), F32)
    for x in range(NX):
        stacked = jnp.concatenate([moved_ref[z * NX + x] for z in range(NZ)], axis=0)
        put = jnp.dot(pick, stacked, preferred_element_type=F32)
        columns = slice(x * width, (x + 1) * width)
        mixed = jnp.where(covered, put, text_ref[:, columns].astype(F32)).T
        rows_ref[columns] = mixed.astype(BF)
        squares += jnp.sum(mixed * mixed, axis=0, keepdims=True)
    squares_ref[...] = two_lines(squares)
    for i, copy in enumerate(copies):
        copy.wait()
        put_head(i, order_ref, rows_ref, buf, rest_refs, out_ref.at[i])
        out_ref[i, buf.shape[1] :] = squares_ref[...]


def project_send(order, target, moved, text, first, rest):
    span, features = text.shape
    width = first.shape[1]
    return pl.pallas_call(
        project_send_kernel,
        in_specs=[IN_SMEM] + [IN_VMEM] * 3 + [IN_HBM] + [IN_VMEM] * len(rest),
        out_specs=[IN_VMEM] * 3,
        out_shape=[
            jax.ShapeDtypeStruct((features, span), BF),
            jax.ShapeDtypeStruct((16, span), BF),
            jax.ShapeDtypeStruct((NY, width + 16, span), BF),
        ],
        scratch_shapes=[
            pltpu.VMEM((NY, width, first.shape[2]), BF),
            pltpu.SemaphoreType.DMA((NY,)),
        ],
        compiler_params=pltpu.CompilerParams(vmem_limit_bytes=VMEM_LIMIT),
        cost_estimate=pl.CostEstimate(
            flops=2 * span * features * (width * NY + 2 * span),
            bytes_accessed=2 * NY * width * (features + span),
            transcendentals=0,
        ),
    )(order, target, moved, text, in_hbm(first), *rest)


def project_keep_kernel(order_ref, rows_ref, squares_ref, got_ref, first_ref, *refs):
    rest_refs, out_refs, (buf, sems) = refs[: -NY - 2], refs[-NY - 2 : -2], refs[-2:]
    copies = fetch(order_ref, first_ref, buf, sems)
    width = first_ref.shape[1]
    for i, out_ref in enumerate(out_refs):
        copies[i].wait()
        put_head(i, order_ref, rows_ref, buf, rest_refs, out_ref, got_ref)
        squares = squares_ref[...].astype(F32) + got_ref[i, width:].astype(F32)
        out_ref[width:] = two_lines(squares[0:1] + squares[1:2])


def project_keep(order, rows, squares, first, rest, got):
    features, span = rows.shape
    width = first.shape[1]
    return pl.pallas_call(
        project_keep_kernel,
        in_specs=[IN_SMEM] + [IN_VMEM] * 3 + [IN_HBM] + [IN_VMEM] * len(rest),
        out_specs=[IN_VMEM] * NY,
        out_shape=[jax.ShapeDtypeStruct((width + 16, span), BF)] * NY,
        scratch_shapes=[
            pltpu.VMEM((NY, width, first.shape[2]), BF),
            pltpu.SemaphoreType.DMA((NY,)),
        ],
        compiler_params=pltpu.CompilerParams(vmem_limit_bytes=VMEM_LIMIT),
        cost_estimate=pl.CostEstimate(
            flops=2 * span * features * width * NY,
            bytes_accessed=2 * NY * width * (features + 2 * span),
            transcendentals=0,
        ),
    )(order, rows, squares, got, in_hbm(first), *rest)


def finish_kernel(features, a, b, c, d, cos_ref, sin_ref, keys_ref, values_ref):
    head = keys_ref.shape[1]
    half = head // 2
    total = a[...].astype(F32)
    for part in (b, c, d):
        total = total + part[...].astype(F32)
    squares = total[2 * head : 2 * head + 1] + total[2 * head + 1 : 2 * head + 2]
    scale = lax.rsqrt(squares / features + EPS)
    lower, upper = total[:half] * scale, total[half:head] * scale
    cos, sin = cos_ref[...], sin_ref[...]
    turned = jnp.concatenate([lower * cos - upper * sin, upper * cos + lower * sin], axis=0)
    keys_ref[...] = turned.T.astype(BF)
    values_ref[...] = (total[head : 2 * head] * scale).T.astype(BF)


def finish(features, parts, cos, sin):
    half, span = cos.shape
    return pl.pallas_call(
        functools.partial(finish_kernel, features),
        out_shape=[jax.ShapeDtypeStruct((span, 2 * half), BF)] * 2,
        compiler_params=pltpu.CompilerParams(vmem_limit_bytes=VMEM_LIMIT),
    )(*parts, cos, sin)


def rotary(positions, head):
    half = head // 2
    frequency = THETA ** (-jnp.arange(half, dtype=F32) * 2.0 / head)
    angles = frequency[:, None] * positions[None, :]
    return jnp.cos(angles), jnp.sin(angles)


def body(
    patches,
    slot_page,
    page_start,
    patch_gain,
    patch_bias,
    merge_in,
    merge_out,
    text,
    norm_gain,
    kv_weight,
):
    enc_index, tp_index = lax.axis_index("enc"), lax.axis_index("tp")
    z_index, x_index = enc_index // NX, enc_index % NX
    y_index, core = tp_index // NC, tp_index % NC
    slots, page_rows, _ = patches.shape
    pages = page_start.shape[0]
    span, features = text.shape
    chunk = page_rows // NZ

    scaled = (kv_weight.T.astype(F32) * norm_gain[None, :]).astype(BF)
    depth, wide = merge_out.shape
    quarter = scaled.shape[0]
    first = features - TAILS * wide
    tail = [scaled[:, first + i * wide : first + (i + 1) * wide] for i in range(TAILS)]
    weights = lax.all_gather(
        jnp.concatenate([merge_out, *tail], axis=0), "enc", axis_index_groups=GROUPS_Z
    )
    scaled = scaled[:, :first]

    hidden = hidden_rows(patches, patch_gain, patch_bias, merge_in)
    dealt = lax.all_to_all(hidden, "enc", 0, 0, axis_index_groups=GROUPS_Z, tiled=True)
    pieces = [dealt] + [lax.ppermute(dealt, "enc", shift_x(d)) for d in range(1, NX)]

    scaled, hidden = lax.optimization_barrier((scaled, hidden))
    by_x = [scaled] + [lax.ppermute(scaled, "enc", shift_x(-d)) for d in range(1, NX)]
    kv_first = lax.all_gather(jnp.concatenate(by_x), "enc", axis_index_groups=GROUPS_Z)

    page_ids = jnp.arange(pages, dtype=jnp.int32)
    slot_ids = jnp.arange(slot_page.shape[0], dtype=jnp.int32)
    slot_of = jnp.sum(
        jnp.where(slot_page[None, :] == page_ids[:, None], slot_ids[None, :], 0), axis=1
    )
    holder = slot_of // slots
    place = (x_index - holder % NX) % NX * NZ + holder // NX
    place = (place * slots + slot_of % slots) * chunk
    target = (place[:, None] + jnp.arange(chunk, dtype=jnp.int32)[None, :]).reshape(-1, 1)

    shifted = (y_index + jnp.arange(NY, dtype=jnp.int32)) % NY * NC
    live, away = send_parts(shifted + (1 - core), target, pieces, weights)
    got = lax.ppermute(away, "tp", SWAP_CORE)
    parts = keep_parts(shifted + core, live, weights, got)
    rest, *parts = lax.optimization_barrier((weights[:, depth:], *parts))
    others = [lax.ppermute(parts[d], "tp", shift_y(d)) for d in range(1, NY)]
    after, before = (lax.ppermute(rest, "enc", shift_x(d)) for d in (-1, 1))
    *others, after, before = lax.optimization_barrier((*others, after, before))
    total = parts[0].astype(F32)
    for other in others:
        total = total + other.astype(F32)
    merged = total.astype(BF)
    across = [
        lax.ppermute(after[:, :quarter], "enc", shift_x(-1)),
        lax.ppermute(before[:, quarter:], "enc", shift_x(1)),
    ]
    kv_rest = [
        rest[:, :quarter],
        rest[:, quarter:],
        after[:, :quarter],
        after[:, quarter:],
        *across,
        before[:, :quarter],
        before[:, quarter:],
    ]

    moved = lax.all_to_all(merged, "enc", 0, 0, tiled=True)
    per_block = pages // (NZ * NX)
    moved = moved.reshape(NZ * NX, per_block * chunk, merged.shape[1])
    starts = lax.dynamic_slice_in_dim(page_start, enc_index * per_block, per_block)
    starts = starts - enc_index * span
    rows = (
        jnp.arange(NZ, dtype=jnp.int32)[:, None, None] * chunk
        + starts[None, :, None]
        + jnp.arange(chunk, dtype=jnp.int32)[None, None, :]
    ).reshape(1, -1)
    order = jnp.concatenate([shifted, (jnp.arange(NX, dtype=jnp.int32) + x_index) % NX])
    turn = jnp.arange(2 * NY, dtype=jnp.int32) < NY
    own_heads = order + jnp.where(turn, core, 0)
    other_heads = order + jnp.where(turn, 1 - core, 0)
    mixed, squares, away = project_send(other_heads, rows, moved, text, kv_first, kv_rest)
    got = lax.ppermute(away, "tp", SWAP_CORE)
    sums = project_keep(own_heads, mixed, squares, kv_first, kv_rest, got)
    sums = [sums[0]] + [lax.ppermute(sums[d], "tp", shift_y(d)) for d in range(1, NY)]

    positions = (enc_index * span + jnp.arange(span, dtype=jnp.int32)).astype(F32)
    cos, sin = rotary(positions, kv_first.shape[1] // 2)
    return tuple(finish(features * NY * NC, sums, cos, sin))


def solution(mesh):
    return jax.shard_map(
        body,
        mesh=mesh,
        in_specs=(
            P(("rep", "enc"), None, None),
            P("rep"),
            P("rep"),
            P(),
            P(),
            P(None, "tp"),
            P("tp", "enc"),
            P(("rep", "enc"), "tp"),
            P("tp"),
            P("tp", "enc"),
        ),
        out_specs=(P(("rep", "enc"), "tp"), P(("rep", "enc"), "tp")),
        check_vma=False,
    )
```

```python
import functools

import jax
import jax.numpy as jnp
from jax import lax
from jax.experimental import pallas as pl
from jax.experimental.pallas import tpu as pltpu
from jax.sharding import PartitionSpec as P

EPS = 1e-06
THETA = 1000000.0
NZ, NX, NY, NC = 8, 4, 4, 2
VMEM_LIMIT = 24 * 1024 * 1024
BF = jnp.bfloat16
F32 = jnp.float32

GROUPS_Z = [[z * NX + x for z in range(NZ)] for x in range(NX)]


def shift_x(d):
    return [(z * NX + x, z * NX + (x + d) % NX) for z in range(NZ) for x in range(NX)]


def shift_z(d):
    return [(z * NX + x, (z + d) % NZ * NX + x) for z in range(NZ) for x in range(NX)]


def shift_y(d):
    return [(y * NC + c, (y + d) % NY * NC + c) for y in range(NY) for c in range(NC)]


SWAP_CORE = [(t, t ^ 1) for t in range(NY * NC)]


IN_VMEM = pl.BlockSpec(memory_space=pltpu.VMEM)
IN_SMEM = pl.BlockSpec(memory_space=pltpu.SMEM)
IN_HBM = pl.BlockSpec(memory_space=pltpu.HBM)


def in_hbm(array):
    return pltpu.with_memory_space_constraint(array, pltpu.HBM)


def hidden_kernel(
    slots,
    patch_ref,
    gain_ref,
    bias_ref,
    weight_ref,
    out_ref,
    patch_buf,
    weight_buf,
    gain_buf,
    bias_buf,
    sems,
):
    width = weight_buf.shape[1]
    groups = weight_buf.shape[0]
    small = (
        pltpu.make_async_copy(gain_ref, gain_buf, sems.at[0, groups]),
        pltpu.make_async_copy(bias_ref, bias_buf, sems.at[1, groups]),
    )
    for copy in small:
        copy.start()
    copies = []
    for i in range(groups):
        part = pl.ds(i * width, width)
        pair = (
            pltpu.make_async_copy(patch_ref.at[:, part], patch_buf.at[i], sems.at[0, i]),
            pltpu.make_async_copy(weight_ref.at[part], weight_buf.at[i], sems.at[1, i]),
        )
        for copy in pair:
            copy.start()
        copies.append(pair)
    for copy in small:
        copy.wait()
    gain, bias = gain_buf[...][None, :], bias_buf[...][None, :]
    total = None
    for i, pair in enumerate(copies):
        pair[0].wait()
        part = patch_buf[i].astype(F32)
        center = jnp.mean(part, axis=-1, keepdims=True)
        part = part - center
        spread = jnp.mean(part * part, axis=-1, keepdims=True)
        normed = (part * lax.rsqrt(spread + EPS) * gain + bias).astype(BF)
        pair[1].wait()
        term = jnp.dot(normed, weight_buf[i], preferred_element_type=F32)
        total = term if total is None else total + term
    total = 0.5 * total * (1.0 + lax.erf(total * 0.7071067811865476))
    rows = total.shape[0] // slots
    chunk = rows // NZ
    pieces = [
        total[slot * rows + z * chunk : slot * rows + (z + 1) * chunk]
        for z in range(NZ)
        for slot in range(slots)
    ]
    out_ref[...] = jnp.concatenate(pieces, axis=0).astype(BF)


def hidden_rows(patches, patch_gain, patch_bias, merge_in):
    slots, rows, feature = patches.shape
    width = patch_gain.shape[0]
    groups = feature // width
    flat = patches.reshape(slots * rows, feature)
    out_width = merge_in.shape[1]
    return pl.pallas_call(
        functools.partial(hidden_kernel, slots),
        in_specs=[IN_HBM] * 4,
        out_specs=IN_VMEM,
        out_shape=jax.ShapeDtypeStruct((slots * rows, out_width), BF),
        scratch_shapes=[
            pltpu.VMEM((groups, slots * rows, width), BF),
            pltpu.VMEM((groups, width, out_width), BF),
            pltpu.VMEM((width,), F32),
            pltpu.VMEM((width,), F32),
            pltpu.SemaphoreType.DMA((2, groups + 1)),
        ],
        compiler_params=pltpu.CompilerParams(vmem_limit_bytes=VMEM_LIMIT),
    )(in_hbm(flat), in_hbm(patch_gain), in_hbm(patch_bias), in_hbm(merge_in))


def live_kernel(target_ref, a, b, c, d, live_ref):
    target = target_ref[...]
    total = None
    for index, piece in enumerate((a, b, c, d)):
        rows = piece.shape[0]
        place = lax.broadcasted_iota(jnp.int32, (target.shape[0], rows), 1) + index * rows
        pick = jnp.where(place == target, 1.0, 0.0).astype(BF)
        term = jnp.dot(pick, piece[...], preferred_element_type=F32)
        total = term if total is None else total + term
    live_ref[...] = total.astype(BF)


def live_rows(target, pieces):
    rows, depth = target.shape[0], pieces[0].shape[1]
    return pl.pallas_call(
        live_kernel,
        out_shape=jax.ShapeDtypeStruct((rows, depth), BF),
        compiler_params=pltpu.CompilerParams(vmem_limit_bytes=VMEM_LIMIT),
    )(target, *pieces)


def fetch_rows(blocks, r, start, rows, target, sems):
    if r == NZ // 2:
        cut = blocks[r].shape[0]
        spans = []
        if start < cut:
            spans.append((blocks[r], start, 0, min(rows, cut - start)))
        if start + rows > cut:
            skip = max(cut - start, 0)
            spans.append((blocks[r + 1], start + skip - cut, skip, rows - skip))
    else:
        spans = [(blocks[r if r < NZ // 2 else r + 1], start, 0, rows)]
    copies = [
        pltpu.make_async_copy(
            ref.at[pl.ds(at, count)], target.at[pl.ds(to, count)], sems.at[index]
        )
        for index, (ref, at, to, count) in enumerate(spans)
    ]
    for copy in copies:
        copy.start()
    return copies


def send_kernel(plan_ref, live_ref, *refs):
    depth = live_ref.shape[1]
    blocks, (out_ref, low_ref, high_ref, buf, sems, kv_sems) = refs[:-6], refs[-6:]
    half = low_ref.shape[1]
    copies = []
    for r in range(NZ):
        copies += fetch_rows(blocks, r, depth, half, low_ref.at[r], kv_sems.at[0, r])
        copies += fetch_rows(blocks, r, depth + half, half, high_ref.at[r], kv_sems.at[1, r])
    for side in range(NC):

        @pl.when(plan_ref[0] == side)
        def _(side=side):
            groups = [
                fetch_rows(blocks, NC * j + side, 0, depth, buf.at[j], sems.at[j])
                for j in range(NY)
            ]
            for j, group in enumerate(groups):
                for copy in group:
                    copy.wait()
                part = jnp.dot(live_ref[...], buf[j], preferred_element_type=F32)
                out_ref[plan_ref[1 + j]] = part.astype(BF)

    for copy in copies:
        copy.wait()


def send_parts(plan, live, blocks):
    rows, depth = live.shape
    total, width = blocks[0].shape
    half = (total - depth) // 2
    return pl.pallas_call(
        send_kernel,
        in_specs=[IN_SMEM, IN_VMEM] + [IN_HBM] * len(blocks),
        out_specs=[IN_VMEM, IN_HBM, IN_HBM],
        out_shape=[jax.ShapeDtypeStruct((NY, rows, width), BF)]
        + [jax.ShapeDtypeStruct((NZ, half, width), BF)] * 2,
        scratch_shapes=[
            pltpu.VMEM((NY, depth, width), BF),
            pltpu.SemaphoreType.DMA((NY, 2)),
            pltpu.SemaphoreType.DMA((2, NZ, 2)),
        ],
        compiler_params=pltpu.CompilerParams(vmem_limit_bytes=VMEM_LIMIT),
    )(plan, live, *[in_hbm(block) for block in blocks])


def keep_kernel(plan_ref, live_ref, got_ref, *refs):
    depth = live_ref.shape[1]
    blocks, out_refs, (buf, sems) = refs[: -NY - 2], refs[-NY - 2 : -2], refs[-2:]
    for side in range(NC):

        @pl.when(plan_ref[0] == side)
        def _(side=side):
            groups = [
                fetch_rows(
                    blocks, NC * j + side, 0, depth, buf.at[plan_ref[1 + j]], sems.at[j]
                )
                for j in range(NY)
            ]
            for group in groups:
                for copy in group:
                    copy.wait()

    for d, out_ref in enumerate(out_refs):
        own = jnp.dot(live_ref[...], buf[d], preferred_element_type=F32).astype(BF)
        out_ref[...] = (own.astype(F32) + got_ref[d].astype(F32)).astype(BF)


def keep_parts(plan, live, got, blocks):
    rows, depth = live.shape
    width = blocks[0].shape[1]
    return pl.pallas_call(
        keep_kernel,
        in_specs=[IN_SMEM, IN_VMEM, IN_VMEM] + [IN_HBM] * len(blocks),
        out_specs=[IN_VMEM] * NY,
        out_shape=[jax.ShapeDtypeStruct((rows, width), BF)] * NY,
        scratch_shapes=[
            pltpu.VMEM((NY, depth, width), BF),
            pltpu.SemaphoreType.DMA((NY, 2)),
        ],
        compiler_params=pltpu.CompilerParams(vmem_limit_bytes=VMEM_LIMIT),
    )(plan, live, got, *[in_hbm(block) for block in blocks])


def put_head(i, order_ref, rows_ref, weight_refs, out_ref, more=None):
    head = order_ref[i]
    rows = weight_refs[0].shape[2] // NX
    lines = []
    for d in range(NX):
        line = [
            ref[head, j * rows : (j + 1) * rows]
            for ref in weight_refs[2 * d : 2 * d + 2]
            for j in range(ref.shape[1] // rows)
        ]
        lines.append(jnp.concatenate(line, axis=1))
    part = jnp.dot(
        jnp.concatenate(lines, axis=0), rows_ref[...], preferred_element_type=F32
    ).astype(BF)
    for d in range(NX):
        place = pl.ds(pl.multiple_of(order_ref[NY + d] * rows, rows), rows)
        piece = part[d * rows : (d + 1) * rows]
        if more is not None:
            piece = (piece.astype(F32) + more[i, place].astype(F32)).astype(BF)
        out_ref[place] = piece


def two_lines(squares):
    squares = jnp.broadcast_to(squares, (16, squares.shape[1]))
    high = squares.astype(BF).astype(F32)
    line = lax.broadcasted_iota(jnp.int32, squares.shape, 0)
    return jnp.where(line == 0, high, jnp.where(line == 1, squares - high, 0.0)).astype(BF)


def project_send_kernel(order_ref, target_ref, moved_ref, text_ref, *refs):
    weight_refs, (rows_ref, squares_ref, out_ref, text_buf, sem) = refs[:-5], refs[-5:]
    text_copy = pltpu.make_async_copy(text_ref, text_buf, sem)
    text_copy.start()
    span = text_ref.shape[0]
    target = target_ref[...]
    place = lax.broadcasted_iota(jnp.int32, (span, target.shape[1]), 0) == target
    pick = jnp.where(place, 1.0, 0.0)
    covered = jnp.sum(pick, axis=1, keepdims=True) > 0.5
    pick = pick.astype(BF)
    width = moved_ref.shape[2]
    squares = jnp.zeros((1, span), F32)
    text_copy.wait()
    for x in range(NX):
        stacked = jnp.concatenate([moved_ref[z * NX + x] for z in range(NZ)], axis=0)
        put = jnp.dot(pick, stacked, preferred_element_type=F32)
        columns = slice(x * width, (x + 1) * width)
        mixed = jnp.where(covered, put, text_buf[:, columns].astype(F32)).T
        rows_ref[columns] = mixed.astype(BF)
        squares += jnp.sum(mixed * mixed, axis=0, keepdims=True)
    squares_ref[...] = two_lines(squares)
    width = weight_refs[0].shape[2]
    for i in range(NY):
        put_head(i, order_ref, rows_ref, weight_refs, out_ref.at[i])
        out_ref[i, width:] = squares_ref[...]


def project_send(order, target, moved, text, weights):
    span, features = text.shape
    width = weights[0].shape[2]
    return pl.pallas_call(
        project_send_kernel,
        in_specs=[IN_SMEM, IN_VMEM, IN_VMEM, IN_HBM] + [IN_VMEM] * len(weights),
        out_specs=[IN_VMEM] * 3,
        out_shape=[
            jax.ShapeDtypeStruct((features, span), BF),
            jax.ShapeDtypeStruct((16, span), BF),
            jax.ShapeDtypeStruct((NY, width + 16, span), BF),
        ],
        scratch_shapes=[pltpu.VMEM((span, features), BF), pltpu.SemaphoreType.DMA(())],
        compiler_params=pltpu.CompilerParams(vmem_limit_bytes=VMEM_LIMIT),
    )(order, target, moved, in_hbm(text), *weights)


def project_keep_kernel(order_ref, rows_ref, squares_ref, got_ref, *refs):
    weight_refs, out_refs = refs[:-NY], refs[-NY:]
    width = weight_refs[0].shape[2]
    for i, out_ref in enumerate(out_refs):
        put_head(i, order_ref, rows_ref, weight_refs, out_ref, got_ref)
        squares = squares_ref[...].astype(F32) + got_ref[i, width:].astype(F32)
        out_ref[width:] = two_lines(squares[0:1] + squares[1:2])


def project_keep(order, rows, squares, got, weights):
    features, span = rows.shape
    width = weights[0].shape[2]
    return pl.pallas_call(
        project_keep_kernel,
        in_specs=[IN_SMEM] + [IN_VMEM] * (3 + len(weights)),
        out_specs=[IN_VMEM] * NY,
        out_shape=[jax.ShapeDtypeStruct((width + 16, span), BF)] * NY,
        compiler_params=pltpu.CompilerParams(vmem_limit_bytes=VMEM_LIMIT),
    )(order, rows, squares, got, *weights)


def finish_kernel(features, a, b, c, d, cos_ref, sin_ref, keys_ref, values_ref):
    head = keys_ref.shape[1]
    half = head // 2
    total = a[...].astype(F32)
    for part in (b, c, d):
        total = total + part[...].astype(F32)
    squares = total[2 * head : 2 * head + 1] + total[2 * head + 1 : 2 * head + 2]
    scale = lax.rsqrt(squares / features + EPS)
    lower, upper = total[:half] * scale, total[half:head] * scale
    cos, sin = cos_ref[...], sin_ref[...]
    turned = jnp.concatenate([lower * cos - upper * sin, upper * cos + lower * sin], axis=0)
    keys_ref[...] = turned.T.astype(BF)
    values_ref[...] = (total[head : 2 * head] * scale).T.astype(BF)


def finish(features, parts, cos, sin):
    half, span = cos.shape
    return pl.pallas_call(
        functools.partial(finish_kernel, features),
        out_shape=[jax.ShapeDtypeStruct((span, 2 * half), BF)] * 2,
        compiler_params=pltpu.CompilerParams(vmem_limit_bytes=VMEM_LIMIT),
    )(*parts, cos, sin)


def rotary(positions, head):
    half = head // 2
    frequency = THETA ** (-jnp.arange(half, dtype=F32) * 2.0 / head)
    angles = frequency[:, None] * positions[None, :]
    return jnp.cos(angles), jnp.sin(angles)


def body(
    patches,
    slot_page,
    page_start,
    patch_gain,
    patch_bias,
    merge_in,
    merge_out,
    text,
    norm_gain,
    kv_weight,
):
    enc_index, tp_index = lax.axis_index("enc"), lax.axis_index("tp")
    z_index, x_index = enc_index // NX, enc_index % NX
    y_index, core = tp_index // NC, tp_index % NC
    slots, page_rows, _ = patches.shape
    pages = page_start.shape[0]
    span, features = text.shape
    chunk = page_rows // NZ

    depth, wide = merge_out.shape
    scaled = (kv_weight.T.astype(F32) * norm_gain[None, :]).astype(BF)
    tails = [scaled[:, i : i + wide] for i in range(0, features, wide)]
    block = jnp.concatenate([merge_out, *tails], axis=0)
    middle = block.shape[0] // 2
    up = [block, lax.ppermute(block, "enc", shift_z(-1))]
    down = [block, lax.ppermute(block, "enc", shift_z(1))]
    hidden = hidden_rows(patches, patch_gain, patch_bias, merge_in)
    hidden, up[1], down[1] = lax.optimization_barrier((hidden, up[1], down[1]))
    for _ in range(NZ // 2 - 2):
        up.append(lax.ppermute(up[-1], "enc", shift_z(-1)))
        down.append(lax.ppermute(down[-1], "enc", shift_z(1)))

    dealt = lax.all_to_all(hidden, "enc", 0, 0, axis_index_groups=GROUPS_Z, tiled=True)
    pieces = [dealt] + [lax.ppermute(dealt, "enc", shift_x(d)) for d in range(1, NX)]
    pieces[1], up[-1], down[-1] = lax.optimization_barrier((pieces[1], up[-1], down[-1]))
    far = [
        lax.ppermute(up[-1][:middle], "enc", shift_z(-1)),
        lax.ppermute(down[-1][middle:], "enc", shift_z(1)),
    ]
    blocks = up + far + down[:0:-1]

    page_ids = jnp.arange(pages, dtype=jnp.int32)
    slot_ids = jnp.arange(slot_page.shape[0], dtype=jnp.int32)
    slot_of = jnp.sum(
        jnp.where(slot_page[None, :] == page_ids[:, None], slot_ids[None, :], 0), axis=1
    )
    holder = slot_of // slots
    place = (x_index - holder % NX) % NX * NZ + holder // NX
    place = (place * slots + slot_of % slots) * chunk
    target = (place[:, None] + jnp.arange(chunk, dtype=jnp.int32)[None, :]).reshape(-1, 1)

    live = live_rows(target, pieces)
    side = (z_index + core) % NC
    steps = jnp.arange(NY, dtype=jnp.int32) * NC

    def plan(side):
        owner = (z_index + steps + side) % NZ // NC
        return jnp.concatenate([side[None], (owner - y_index) % NY])

    away, *kv_own = send_parts(plan(1 - side), live, blocks)
    got = lax.ppermute(away, "tp", SWAP_CORE)
    after = [lax.ppermute(part, "enc", shift_x(-1)) for part in kv_own]
    before = [lax.ppermute(part, "enc", shift_x(1)) for part in kv_own]
    parts = keep_parts(plan(side), live, got, blocks)
    others = [lax.ppermute(parts[d], "tp", shift_y(d)) for d in range(1, NY)]
    opposite = [
        lax.ppermute(after[0], "enc", shift_x(-1)),
        lax.ppermute(before[1], "enc", shift_x(1)),
    ]
    total = parts[0].astype(F32)
    for other in others:
        total = total + other.astype(F32)
    merged = total.astype(BF)
    kv_all = [*kv_own, *after, *opposite, *before]

    moved = lax.all_to_all(merged, "enc", 0, 0, tiled=True)
    per_block = pages // (NZ * NX)
    moved = moved.reshape(NZ * NX, per_block * chunk, merged.shape[1])
    starts = lax.dynamic_slice_in_dim(page_start, enc_index * per_block, per_block)
    starts = starts - enc_index * span
    rows = (
        jnp.arange(NZ, dtype=jnp.int32)[:, None, None] * chunk
        + starts[None, :, None]
        + jnp.arange(chunk, dtype=jnp.int32)[None, None, :]
    ).reshape(1, -1)
    shifted = (y_index + jnp.arange(NY, dtype=jnp.int32)) % NY * NC
    order = jnp.concatenate([shifted - z_index, (jnp.arange(NX, dtype=jnp.int32) + x_index) % NX])
    turn = jnp.arange(2 * NY, dtype=jnp.int32) < NY
    own_heads = jnp.where(turn, (order + core) % NZ, order)
    other_heads = jnp.where(turn, (order + 1 - core) % NZ, order)
    mixed, squares, away = project_send(other_heads, rows, moved, text, kv_all)
    got = lax.ppermute(away, "tp", SWAP_CORE)
    sums = project_keep(own_heads, mixed, squares, got, kv_all)
    sums = [sums[0]] + [lax.ppermute(sums[d], "tp", shift_y(d)) for d in range(1, NY)]

    positions = (enc_index * span + jnp.arange(span, dtype=jnp.int32)).astype(F32)
    cos, sin = rotary(positions, wide // 2)
    return tuple(finish(features * NY * NC, sums, cos, sin))


def solution(mesh):
    return jax.shard_map(
        body,
        mesh=mesh,
        in_specs=(
            P(("rep", "enc"), None, None),
            P("rep"),
            P("rep"),
            P(),
            P(),
            P(None, "tp"),
            P("tp", "enc"),
            P(("rep", "enc"), "tp"),
            P("tp"),
            P("tp", "enc"),
        ),
        out_specs=(P(("rep", "enc"), "tp"), P(("rep", "enc"), "tp")),
        check_vma=False,
    )
```

```python
import functools

import jax
import jax.numpy as jnp
from jax import lax
from jax.experimental import pallas as pl
from jax.experimental.pallas import tpu as pltpu
from jax.sharding import PartitionSpec as P

EPS = 1e-06
THETA = 1000000.0
NZ, NX, NY, NC = 8, 4, 4, 2
VMEM_LIMIT = 24 * 1024 * 1024
BF = jnp.bfloat16
F32 = jnp.float32

GROUPS_Z = [[z * NX + x for z in range(NZ)] for x in range(NX)]


def shift_x(d):
    return [(z * NX + x, z * NX + (x + d) % NX) for z in range(NZ) for x in range(NX)]


def shift_z(d):
    return [(z * NX + x, (z + d) % NZ * NX + x) for z in range(NZ) for x in range(NX)]


def shift_y(d):
    return [(y * NC + c, (y + d) % NY * NC + c) for y in range(NY) for c in range(NC)]


SWAP_CORE = [(t, t ^ 1) for t in range(NY * NC)]


IN_VMEM = pl.BlockSpec(memory_space=pltpu.VMEM)
IN_SMEM = pl.BlockSpec(memory_space=pltpu.SMEM)
IN_HBM = pl.BlockSpec(memory_space=pltpu.HBM)


def in_hbm(array):
    return pltpu.with_memory_space_constraint(array, pltpu.HBM)


def hidden_kernel(
    slots,
    patch_ref,
    gain_ref,
    bias_ref,
    weight_ref,
    out_ref,
    patch_buf,
    weight_buf,
    gain_buf,
    bias_buf,
    sems,
):
    width = weight_buf.shape[1]
    groups = weight_buf.shape[0]
    small = (
        pltpu.make_async_copy(gain_ref, gain_buf, sems.at[0, groups]),
        pltpu.make_async_copy(bias_ref, bias_buf, sems.at[1, groups]),
    )
    for copy in small:
        copy.start()
    copies = []
    for i in range(groups):
        part = pl.ds(i * width, width)
        pair = (
            pltpu.make_async_copy(patch_ref.at[:, part], patch_buf.at[i], sems.at[0, i]),
            pltpu.make_async_copy(weight_ref.at[part], weight_buf.at[i], sems.at[1, i]),
        )
        for copy in pair:
            copy.start()
        copies.append(pair)
    for copy in small:
        copy.wait()
    gain, bias = gain_buf[...][None, :], bias_buf[...][None, :]
    total = None
    for i, pair in enumerate(copies):
        pair[0].wait()
        part = patch_buf[i].astype(F32)
        center = jnp.mean(part, axis=-1, keepdims=True)
        part = part - center
        spread = jnp.mean(part * part, axis=-1, keepdims=True)
        normed = (part * lax.rsqrt(spread + EPS) * gain + bias).astype(BF)
        pair[1].wait()
        term = jnp.dot(normed, weight_buf[i], preferred_element_type=F32)
        total = term if total is None else total + term
    total = 0.5 * total * (1.0 + lax.erf(total * 0.7071067811865476))
    rows = total.shape[0] // slots
    chunk = rows // NZ
    pieces = [
        total[slot * rows + z * chunk : slot * rows + (z + 1) * chunk]
        for z in range(NZ)
        for slot in range(slots)
    ]
    out_ref[...] = jnp.concatenate(pieces, axis=0).astype(BF)


def hidden_rows(patches, patch_gain, patch_bias, merge_in):
    slots, rows, feature = patches.shape
    width = patch_gain.shape[0]
    groups = feature // width
    flat = patches.reshape(slots * rows, feature)
    out_width = merge_in.shape[1]
    return pl.pallas_call(
        functools.partial(hidden_kernel, slots),
        in_specs=[IN_HBM] * 4,
        out_specs=IN_VMEM,
        out_shape=jax.ShapeDtypeStruct((slots * rows, out_width), BF),
        scratch_shapes=[
            pltpu.VMEM((groups, slots * rows, width), BF),
            pltpu.VMEM((groups, width, out_width), BF),
            pltpu.VMEM((width,), F32),
            pltpu.VMEM((width,), F32),
            pltpu.SemaphoreType.DMA((2, groups + 1)),
        ],
        compiler_params=pltpu.CompilerParams(vmem_limit_bytes=VMEM_LIMIT),
    )(in_hbm(flat), in_hbm(patch_gain), in_hbm(patch_bias), in_hbm(merge_in))


def live_kernel(target_ref, a, b, c, d, live_ref):
    target = target_ref[...]
    total = None
    for index, piece in enumerate((a, b, c, d)):
        rows = piece.shape[0]
        place = lax.broadcasted_iota(jnp.int32, (target.shape[0], rows), 1) + index * rows
        pick = jnp.where(place == target, 1.0, 0.0).astype(BF)
        term = jnp.dot(pick, piece[...], preferred_element_type=F32)
        total = term if total is None else total + term
    live_ref[...] = total.astype(BF)


def live_rows(target, pieces):
    rows, depth = target.shape[0], pieces[0].shape[1]
    return pl.pallas_call(
        live_kernel,
        out_shape=jax.ShapeDtypeStruct((rows, depth), BF),
        compiler_params=pltpu.CompilerParams(vmem_limit_bytes=VMEM_LIMIT),
    )(target, *pieces)


def fetch_rows(blocks, r, start, rows, target, sems):
    if r == NZ // 2:
        cut = blocks[r].shape[0]
        spans = []
        if start < cut:
            spans.append((blocks[r], start, 0, min(rows, cut - start)))
        if start + rows > cut:
            skip = max(cut - start, 0)
            spans.append((blocks[r + 1], start + skip - cut, skip, rows - skip))
    else:
        spans = [(blocks[r if r < NZ // 2 else r + 1], start, 0, rows)]
    copies = [
        pltpu.make_async_copy(
            ref.at[pl.ds(at, count)], target.at[pl.ds(to, count)], sems.at[index]
        )
        for index, (ref, at, to, count) in enumerate(spans)
    ]
    for copy in copies:
        copy.start()
    return copies


def send_kernel(plan_ref, live_ref, *refs):
    depth = live_ref.shape[1]
    blocks, (out_ref, low_ref, high_ref, kept_ref, buf, sems, kv_sems, kept_sems) = (
        refs[:-8],
        refs[-8:],
    )
    half = low_ref.shape[1]
    copies = []
    for r in range(NZ):
        copies += fetch_rows(blocks, r, depth, half, low_ref.at[r], kv_sems.at[0, r])
        copies += fetch_rows(blocks, r, depth + half, half, high_ref.at[r], kv_sems.at[1, r])
    for side in range(NC):

        @pl.when(plan_ref[0] == side)
        def _(side=side):
            groups = [
                fetch_rows(blocks, NC * j + side, 0, depth, buf.at[j], sems.at[j])
                for j in range(NY)
            ]
            kept = []
            for j in range(NY):
                target = kept_ref.at[plan_ref[1 + NY + j]]
                kept += fetch_rows(
                    blocks, NC * j + 1 - side, 0, depth, target, kept_sems.at[j]
                )
            for j, group in enumerate(groups):
                for copy in group:
                    copy.wait()
                part = jnp.dot(live_ref[...], buf[j], preferred_element_type=F32)
                out_ref[plan_ref[1 + j]] = part.astype(BF)
            for copy in kept:
                copy.wait()

    for copy in copies:
        copy.wait()


def send_parts(plan, live, blocks):
    rows, depth = live.shape
    width = blocks[0].shape[1]
    half = (blocks[0].shape[0] - depth) // 2
    return pl.pallas_call(
        send_kernel,
        in_specs=[IN_SMEM, IN_VMEM] + [IN_HBM] * len(blocks),
        out_specs=[IN_VMEM, IN_HBM, IN_HBM, IN_VMEM],
        out_shape=[jax.ShapeDtypeStruct((NY, rows, width), BF)]
        + [jax.ShapeDtypeStruct((NZ, half, width), BF)] * 2
        + [jax.ShapeDtypeStruct((NY, depth, width), BF)],
        scratch_shapes=[
            pltpu.VMEM((NY, depth, width), BF),
            pltpu.SemaphoreType.DMA((NY, 2)),
            pltpu.SemaphoreType.DMA((2, NZ, 2)),
            pltpu.SemaphoreType.DMA((NY, 2)),
        ],
        compiler_params=pltpu.CompilerParams(vmem_limit_bytes=VMEM_LIMIT),
    )(plan, live, *[in_hbm(block) for block in blocks])


def keep_kernel(live_ref, got_ref, weight_ref, *out_refs):
    for d, out_ref in enumerate(out_refs):
        own = jnp.dot(live_ref[...], weight_ref[d], preferred_element_type=F32).astype(BF)
        out_ref[...] = (own.astype(F32) + got_ref[d].astype(F32)).astype(BF)


def keep_parts(live, got, weights):
    rows, width = live.shape[0], weights.shape[2]
    return pl.pallas_call(
        keep_kernel,
        out_shape=[jax.ShapeDtypeStruct((rows, width), BF)] * NY,
        compiler_params=pltpu.CompilerParams(vmem_limit_bytes=VMEM_LIMIT),
    )(live, got, weights)


def put_head(i, order_ref, rows_ref, weight_refs, out_ref, more=None):
    head = order_ref[i]
    rows = weight_refs[0].shape[2] // NX
    lines = []
    for d in range(NX):
        line = [
            ref[head, j * rows : (j + 1) * rows]
            for ref in weight_refs[2 * d : 2 * d + 2]
            for j in range(ref.shape[1] // rows)
        ]
        lines.append(jnp.concatenate(line, axis=1))
    part = jnp.dot(
        jnp.concatenate(lines, axis=0), rows_ref[...], preferred_element_type=F32
    ).astype(BF)
    for d in range(NX):
        place = pl.ds(pl.multiple_of(order_ref[NY + d] * rows, rows), rows)
        piece = part[d * rows : (d + 1) * rows]
        if more is not None:
            piece = (piece.astype(F32) + more[i, place].astype(F32)).astype(BF)
        out_ref[place] = piece


def two_lines(squares):
    squares = jnp.broadcast_to(squares, (16, squares.shape[1]))
    high = squares.astype(BF).astype(F32)
    line = lax.broadcasted_iota(jnp.int32, squares.shape, 0)
    return jnp.where(line == 0, high, jnp.where(line == 1, squares - high, 0.0)).astype(BF)


def project_send_kernel(order_ref, target_ref, moved_ref, text_ref, *refs):
    weight_refs, (rows_ref, squares_ref, out_ref, text_buf, sem) = refs[:-5], refs[-5:]
    text_copy = pltpu.make_async_copy(text_ref, text_buf, sem)
    text_copy.start()
    span = text_ref.shape[0]
    target = target_ref[...]
    place = lax.broadcasted_iota(jnp.int32, (span, target.shape[1]), 0) == target
    pick = jnp.where(place, 1.0, 0.0)
    covered = jnp.sum(pick, axis=1, keepdims=True) > 0.5
    pick = pick.astype(BF)
    width = moved_ref.shape[2]
    squares = jnp.zeros((1, span), F32)
    text_copy.wait()
    for x in range(NX):
        stacked = jnp.concatenate([moved_ref[z * NX + x] for z in range(NZ)], axis=0)
        put = jnp.dot(pick, stacked, preferred_element_type=F32)
        columns = slice(x * width, (x + 1) * width)
        mixed = jnp.where(covered, put, text_buf[:, columns].astype(F32)).T
        rows_ref[columns] = mixed.astype(BF)
        squares += jnp.sum(mixed * mixed, axis=0, keepdims=True)
    squares_ref[...] = two_lines(squares)
    width = weight_refs[0].shape[2]
    for i in range(NY):
        put_head(i, order_ref, rows_ref, weight_refs, out_ref.at[i])
        out_ref[i, width:] = squares_ref[...]


def project_send(order, target, moved, text, weights):
    span, features = text.shape
    width = weights[0].shape[2]
    return pl.pallas_call(
        project_send_kernel,
        in_specs=[IN_SMEM, IN_VMEM, IN_VMEM, IN_HBM] + [IN_VMEM] * len(weights),
        out_specs=[IN_VMEM] * 3,
        out_shape=[
            jax.ShapeDtypeStruct((features, span), BF),
            jax.ShapeDtypeStruct((16, span), BF),
            jax.ShapeDtypeStruct((NY, width + 16, span), BF),
        ],
        scratch_shapes=[pltpu.VMEM((span, features), BF), pltpu.SemaphoreType.DMA(())],
        compiler_params=pltpu.CompilerParams(vmem_limit_bytes=VMEM_LIMIT),
    )(order, target, moved, in_hbm(text), *weights)


def project_keep_kernel(order_ref, rows_ref, squares_ref, got_ref, *refs):
    weight_refs, out_refs = refs[:-NY], refs[-NY:]
    width = weight_refs[0].shape[2]
    for i, out_ref in enumerate(out_refs):
        put_head(i, order_ref, rows_ref, weight_refs, out_ref, got_ref)
        squares = squares_ref[...].astype(F32) + got_ref[i, width:].astype(F32)
        out_ref[width:] = two_lines(squares[0:1] + squares[1:2])


def project_keep(order, rows, squares, got, weights):
    features, span = rows.shape
    width = weights[0].shape[2]
    return pl.pallas_call(
        project_keep_kernel,
        in_specs=[IN_SMEM] + [IN_VMEM] * (3 + len(weights)),
        out_specs=[IN_VMEM] * NY,
        out_shape=[jax.ShapeDtypeStruct((width + 16, span), BF)] * NY,
        compiler_params=pltpu.CompilerParams(vmem_limit_bytes=VMEM_LIMIT),
    )(order, rows, squares, got, *weights)


def finish_kernel(features, a, b, c, d, cos_ref, sin_ref, keys_ref, values_ref):
    head = keys_ref.shape[1]
    half = head // 2
    total = a[...].astype(F32)
    for part in (b, c, d):
        total = total + part[...].astype(F32)
    squares = total[2 * head : 2 * head + 1] + total[2 * head + 1 : 2 * head + 2]
    scale = lax.rsqrt(squares / features + EPS)
    lower, upper = total[:half] * scale, total[half:head] * scale
    cos, sin = cos_ref[...], sin_ref[...]
    turned = jnp.concatenate([lower * cos - upper * sin, upper * cos + lower * sin], axis=0)
    keys_ref[...] = turned.T.astype(BF)
    values_ref[...] = (total[head : 2 * head] * scale).T.astype(BF)


def finish(features, parts, cos, sin):
    half, span = cos.shape
    return pl.pallas_call(
        functools.partial(finish_kernel, features),
        out_shape=[jax.ShapeDtypeStruct((span, 2 * half), BF)] * 2,
        compiler_params=pltpu.CompilerParams(vmem_limit_bytes=VMEM_LIMIT),
    )(*parts, cos, sin)


def rotary(positions, head):
    half = head // 2
    frequency = THETA ** (-jnp.arange(half, dtype=F32) * 2.0 / head)
    angles = frequency[:, None] * positions[None, :]
    return jnp.cos(angles), jnp.sin(angles)


def body(
    patches,
    slot_page,
    page_start,
    patch_gain,
    patch_bias,
    merge_in,
    merge_out,
    text,
    norm_gain,
    kv_weight,
):
    enc_index, tp_index = lax.axis_index("enc"), lax.axis_index("tp")
    z_index, x_index = enc_index // NX, enc_index % NX
    y_index, core = tp_index // NC, tp_index % NC
    slots, page_rows, _ = patches.shape
    pages = page_start.shape[0]
    span, features = text.shape
    chunk = page_rows // NZ

    depth, wide = merge_out.shape
    scaled = (kv_weight.T.astype(F32) * norm_gain[None, :]).astype(BF)
    tails = [scaled[:, i : i + wide] for i in range(0, features, wide)]
    block = jnp.concatenate([merge_out, *tails], axis=0)
    middle = block.shape[0] // 2
    up = [block, lax.ppermute(block, "enc", shift_z(-1))]
    down = [block, lax.ppermute(block, "enc", shift_z(1))]
    hidden = hidden_rows(patches, patch_gain, patch_bias, merge_in)
    hidden, up[1], down[1] = lax.optimization_barrier((hidden, up[1], down[1]))
    for _ in range(NZ // 2 - 2):
        up.append(lax.ppermute(up[-1], "enc", shift_z(-1)))
        down.append(lax.ppermute(down[-1], "enc", shift_z(1)))

    dealt = lax.all_to_all(hidden, "enc", 0, 0, axis_index_groups=GROUPS_Z, tiled=True)
    pieces = [dealt] + [lax.ppermute(dealt, "enc", shift_x(d)) for d in range(1, NX)]
    pieces[1], up[-1], down[-1] = lax.optimization_barrier((pieces[1], up[-1], down[-1]))
    far = [
        lax.ppermute(up[-1][:middle], "enc", shift_z(-1)),
        lax.ppermute(down[-1][middle:], "enc", shift_z(1)),
    ]
    blocks = up + far + down[:0:-1]

    page_ids = jnp.arange(pages, dtype=jnp.int32)
    slot_ids = jnp.arange(slot_page.shape[0], dtype=jnp.int32)
    slot_of = jnp.sum(
        jnp.where(slot_page[None, :] == page_ids[:, None], slot_ids[None, :], 0), axis=1
    )
    holder = slot_of // slots
    place = (x_index - holder % NX) % NX * NZ + holder // NX
    place = (place * slots + slot_of % slots) * chunk
    target = (place[:, None] + jnp.arange(chunk, dtype=jnp.int32)[None, :]).reshape(-1, 1)

    live = live_rows(target, pieces)
    side = (z_index + core) % NC
    steps = jnp.arange(NY, dtype=jnp.int32) * NC

    def plan(side):
        owner = (z_index + steps + side) % NZ // NC
        return (owner - y_index) % NY

    plan = jnp.concatenate([1 - side[None], plan(1 - side), plan(side)])
    away, *kv_own, kept = send_parts(plan, live, blocks)
    got = lax.ppermute(away, "tp", SWAP_CORE)
    after = [lax.ppermute(part, "enc", shift_x(-1)) for part in kv_own]
    before = [lax.ppermute(part, "enc", shift_x(1)) for part in kv_own]
    parts = keep_parts(live, got, kept)
    others = [lax.ppermute(parts[d], "tp", shift_y(d)) for d in range(1, NY)]
    opposite = [
        lax.ppermute(after[0], "enc", shift_x(-1)),
        lax.ppermute(before[1], "enc", shift_x(1)),
    ]
    total = parts[0].astype(F32)
    for other in others:
        total = total + other.astype(F32)
    merged = total.astype(BF)
    kv_all = [*kv_own, *after, *opposite, *before]

    moved = lax.all_to_all(merged, "enc", 0, 0, tiled=True)
    per_block = pages // (NZ * NX)
    moved = moved.reshape(NZ * NX, per_block * chunk, merged.shape[1])
    starts = lax.dynamic_slice_in_dim(page_start, enc_index * per_block, per_block)
    starts = starts - enc_index * span
    rows = (
        jnp.arange(NZ, dtype=jnp.int32)[:, None, None] * chunk
        + starts[None, :, None]
        + jnp.arange(chunk, dtype=jnp.int32)[None, None, :]
    ).reshape(1, -1)
    shifted = (y_index + jnp.arange(NY, dtype=jnp.int32)) % NY * NC
    order = jnp.concatenate([shifted - z_index, (jnp.arange(NX, dtype=jnp.int32) + x_index) % NX])
    turn = jnp.arange(2 * NY, dtype=jnp.int32) < NY
    own_heads = jnp.where(turn, (order + core) % NZ, order)
    other_heads = jnp.where(turn, (order + 1 - core) % NZ, order)
    mixed, squares, away = project_send(other_heads, rows, moved, text, kv_all)
    got = lax.ppermute(away, "tp", SWAP_CORE)
    sums = project_keep(own_heads, mixed, squares, got, kv_all)
    sums = [sums[0]] + [lax.ppermute(sums[d], "tp", shift_y(d)) for d in range(1, NY)]

    positions = (enc_index * span + jnp.arange(span, dtype=jnp.int32)).astype(F32)
    cos, sin = rotary(positions, wide // 2)
    return tuple(finish(features * NY * NC, sums, cos, sin))


def solution(mesh):
    return jax.shard_map(
        body,
        mesh=mesh,
        in_specs=(
            P(("rep", "enc"), None, None),
            P("rep"),
            P("rep"),
            P(),
            P(),
            P(None, "tp"),
            P("tp", "enc"),
            P(("rep", "enc"), "tp"),
            P("tp"),
            P("tp", "enc"),
        ),
        out_specs=(P(("rep", "enc"), "tp"), P(("rep", "enc"), "tp")),
        check_vma=False,
    )
```

```python
import functools

import jax
import jax.numpy as jnp
from jax import lax
from jax.experimental import pallas as pl
from jax.experimental.pallas import tpu as pltpu
from jax.sharding import PartitionSpec as P

EPS = 1e-06
THETA = 1000000.0
NZ, NX, NY, NC = 8, 4, 4, 2
VMEM_LIMIT = 24 * 1024 * 1024
BF = jnp.bfloat16
F32 = jnp.float32

GROUPS_Z = [[z * NX + x for z in range(NZ)] for x in range(NX)]


def shift_x(d):
    return [(z * NX + x, z * NX + (x + d) % NX) for z in range(NZ) for x in range(NX)]


def shift_z(d):
    return [(z * NX + x, (z + d) % NZ * NX + x) for z in range(NZ) for x in range(NX)]


def shift_y(d):
    return [(y * NC + c, (y + d) % NY * NC + c) for y in range(NY) for c in range(NC)]


SWAP_CORE = [(t, t ^ 1) for t in range(NY * NC)]


IN_VMEM = pl.BlockSpec(memory_space=pltpu.VMEM)
IN_SMEM = pl.BlockSpec(memory_space=pltpu.SMEM)
IN_HBM = pl.BlockSpec(memory_space=pltpu.HBM)


def in_hbm(array):
    return pltpu.with_memory_space_constraint(array, pltpu.HBM)


def hidden_kernel(
    slots,
    patch_ref,
    gain_ref,
    bias_ref,
    weight_ref,
    out_ref,
    patch_buf,
    weight_buf,
    gain_buf,
    bias_buf,
    sems,
):
    width = weight_buf.shape[1]
    groups = weight_buf.shape[0]
    small = (
        pltpu.make_async_copy(gain_ref, gain_buf, sems.at[0, groups]),
        pltpu.make_async_copy(bias_ref, bias_buf, sems.at[1, groups]),
    )
    for copy in small:
        copy.start()
    copies = []
    for i in range(groups):
        part = pl.ds(i * width, width)
        pair = (
            pltpu.make_async_copy(patch_ref.at[:, part], patch_buf.at[i], sems.at[0, i]),
            pltpu.make_async_copy(weight_ref.at[part], weight_buf.at[i], sems.at[1, i]),
        )
        for copy in pair:
            copy.start()
        copies.append(pair)
    for copy in small:
        copy.wait()
    gain, bias = gain_buf[...][None, :], bias_buf[...][None, :]
    total = None
    for i, pair in enumerate(copies):
        pair[0].wait()
        part = patch_buf[i].astype(F32)
        center = jnp.mean(part, axis=-1, keepdims=True)
        part = part - center
        spread = jnp.mean(part * part, axis=-1, keepdims=True)
        normed = (part * lax.rsqrt(spread + EPS) * gain + bias).astype(BF)
        pair[1].wait()
        term = jnp.dot(normed, weight_buf[i], preferred_element_type=F32)
        total = term if total is None else total + term
    total = 0.5 * total * (1.0 + lax.erf(total * 0.7071067811865476))
    rows = total.shape[0] // slots
    chunk = rows // NZ
    pieces = [
        total[slot * rows + z * chunk : slot * rows + (z + 1) * chunk]
        for z in range(NZ)
        for slot in range(slots)
    ]
    out_ref[...] = jnp.concatenate(pieces, axis=0).astype(BF)


def hidden_rows(patches, patch_gain, patch_bias, merge_in):
    slots, rows, feature = patches.shape
    width = patch_gain.shape[0]
    groups = feature // width
    flat = patches.reshape(slots * rows, feature)
    out_width = merge_in.shape[1]
    return pl.pallas_call(
        functools.partial(hidden_kernel, slots),
        in_specs=[IN_HBM] * 4,
        out_specs=IN_VMEM,
        out_shape=jax.ShapeDtypeStruct((slots * rows, out_width), BF),
        scratch_shapes=[
            pltpu.VMEM((groups, slots * rows, width), BF),
            pltpu.VMEM((groups, width, out_width), BF),
            pltpu.VMEM((width,), F32),
            pltpu.VMEM((width,), F32),
            pltpu.SemaphoreType.DMA((2, groups + 1)),
        ],
        compiler_params=pltpu.CompilerParams(vmem_limit_bytes=VMEM_LIMIT),
    )(in_hbm(flat), in_hbm(patch_gain), in_hbm(patch_bias), in_hbm(merge_in))


def live_kernel(target_ref, a, b, c, d, live_ref):
    target = target_ref[...]
    total = None
    for index, piece in enumerate((a, b, c, d)):
        rows = piece.shape[0]
        place = lax.broadcasted_iota(jnp.int32, (target.shape[0], rows), 1) + index * rows
        pick = jnp.where(place == target, 1.0, 0.0).astype(BF)
        term = jnp.dot(pick, piece[...], preferred_element_type=F32)
        total = term if total is None else total + term
    live_ref[...] = total.astype(BF)


def live_rows(target, pieces):
    rows, depth = target.shape[0], pieces[0].shape[1]
    return pl.pallas_call(
        live_kernel,
        out_shape=jax.ShapeDtypeStruct((rows, depth), BF),
        compiler_params=pltpu.CompilerParams(vmem_limit_bytes=VMEM_LIMIT),
    )(target, *pieces)


def fetch_rows(blocks, r, start, rows, target, sems):
    if r == NZ // 2:
        cut = blocks[r].shape[0]
        spans = []
        if start < cut:
            spans.append((blocks[r], start, 0, min(rows, cut - start)))
        if start + rows > cut:
            skip = max(cut - start, 0)
            spans.append((blocks[r + 1], start + skip - cut, skip, rows - skip))
    else:
        spans = [(blocks[r if r < NZ // 2 else r + 1], start, 0, rows)]
    copies = [
        pltpu.make_async_copy(
            ref.at[pl.ds(at, count)], target.at[pl.ds(to, count)], sems.at[index]
        )
        for index, (ref, at, to, count) in enumerate(spans)
    ]
    for copy in copies:
        copy.start()
    return copies


def send_kernel(plan_ref, live_ref, *refs):
    depth = live_ref.shape[1]
    blocks, (out_ref, low_ref, high_ref, kept_ref, buf, sems, kv_sems, kept_sems) = (
        refs[:-8],
        refs[-8:],
    )
    half = low_ref.shape[1]
    copies = []
    for r in range(NZ):
        copies += fetch_rows(blocks, r, depth, half, low_ref.at[r], kv_sems.at[0, r])
        copies += fetch_rows(blocks, r, depth + half, half, high_ref.at[r], kv_sems.at[1, r])
    for side in range(NC):

        @pl.when(plan_ref[0] == side)
        def _(side=side):
            groups = [
                fetch_rows(blocks, NC * j + side, 0, depth, buf.at[j], sems.at[j])
                for j in range(NY)
            ]
            kept = []
            for j in range(NY):
                target = kept_ref.at[plan_ref[1 + NY + j]]
                kept += fetch_rows(
                    blocks, NC * j + 1 - side, 0, depth, target, kept_sems.at[j]
                )
            for j, group in enumerate(groups):
                for copy in group:
                    copy.wait()
                part = jnp.dot(live_ref[...], buf[j], preferred_element_type=F32)
                out_ref[plan_ref[1 + j]] = part.astype(BF)
            for copy in kept:
                copy.wait()

    for copy in copies:
        copy.wait()


def send_parts(plan, live, blocks):
    rows, depth = live.shape
    width = blocks[0].shape[1]
    half = (blocks[0].shape[0] - depth) // 2
    return pl.pallas_call(
        send_kernel,
        in_specs=[IN_SMEM, IN_VMEM] + [IN_HBM] * len(blocks),
        out_specs=[IN_VMEM, IN_HBM, IN_HBM, IN_VMEM],
        out_shape=[jax.ShapeDtypeStruct((NY, rows, width), BF)]
        + [jax.ShapeDtypeStruct((NZ, half, width), BF)] * 2
        + [jax.ShapeDtypeStruct((NY, depth, width), BF)],
        scratch_shapes=[
            pltpu.VMEM((NY, depth, width), BF),
            pltpu.SemaphoreType.DMA((NY, 2)),
            pltpu.SemaphoreType.DMA((2, NZ, 2)),
            pltpu.SemaphoreType.DMA((NY, 2)),
        ],
        compiler_params=pltpu.CompilerParams(vmem_limit_bytes=VMEM_LIMIT),
    )(plan, live, *[in_hbm(block) for block in blocks])


def keep_kernel(live_ref, got_ref, weight_ref, *out_refs):
    for d, out_ref in enumerate(out_refs):
        own = jnp.dot(live_ref[...], weight_ref[d], preferred_element_type=F32).astype(BF)
        out_ref[...] = (own.astype(F32) + got_ref[d].astype(F32)).astype(BF)


def keep_parts(live, got, weights):
    rows, width = live.shape[0], weights.shape[2]
    return pl.pallas_call(
        keep_kernel,
        out_shape=[jax.ShapeDtypeStruct((rows, width), BF)] * NY,
        compiler_params=pltpu.CompilerParams(vmem_limit_bytes=VMEM_LIMIT),
    )(live, got, weights)


def put_head(i, order_ref, rows_ref, weight_refs, out_ref):
    head = order_ref[i]
    rows = weight_refs[0].shape[2] // NX
    lines = []
    for d in range(NX):
        line = [
            ref[head, j * rows : (j + 1) * rows]
            for ref in weight_refs[2 * d : 2 * d + 2]
            for j in range(ref.shape[1] // rows)
        ]
        lines.append(jnp.concatenate(line, axis=1))
    part = jnp.dot(
        jnp.concatenate(lines, axis=0), rows_ref[...], preferred_element_type=F32
    ).astype(BF)
    for d in range(NX):
        place = pl.ds(pl.multiple_of(order_ref[NY + d] * rows, rows), rows)
        out_ref[place] = part[d * rows : (d + 1) * rows]


def two_lines(squares):
    squares = jnp.broadcast_to(squares, (16, squares.shape[1]))
    high = squares.astype(BF).astype(F32)
    line = lax.broadcasted_iota(jnp.int32, squares.shape, 0)
    return jnp.where(line == 0, high, jnp.where(line == 1, squares - high, 0.0)).astype(BF)


def mix_kernel(target_ref, moved_ref, text_ref, rows_ref, squares_ref, text_buf, sem):
    text_copy = pltpu.make_async_copy(text_ref, text_buf, sem)
    text_copy.start()
    span = text_ref.shape[0]
    target = target_ref[...]
    place = lax.broadcasted_iota(jnp.int32, (span, target.shape[1]), 0) == target
    pick = jnp.where(place, 1.0, 0.0)
    covered = jnp.sum(pick, axis=1, keepdims=True) > 0.5
    pick = pick.astype(BF)
    width = moved_ref.shape[2]
    squares = jnp.zeros((1, span), F32)
    text_copy.wait()
    for x in range(NX):
        stacked = jnp.concatenate([moved_ref[z * NX + x] for z in range(NZ)], axis=0)
        put = jnp.dot(pick, stacked, preferred_element_type=F32)
        columns = slice(x * width, (x + 1) * width)
        mixed = jnp.where(covered, put, text_buf[:, columns].astype(F32)).T
        rows_ref[columns] = mixed.astype(BF)
        squares += jnp.sum(mixed * mixed, axis=0, keepdims=True)
    squares_ref[...] = two_lines(squares)


def mix(target, moved, text):
    span, features = text.shape
    return pl.pallas_call(
        mix_kernel,
        in_specs=[IN_VMEM, IN_VMEM, IN_HBM],
        out_specs=[IN_VMEM] * 2,
        out_shape=[
            jax.ShapeDtypeStruct((features, span), BF),
            jax.ShapeDtypeStruct((16, span), BF),
        ],
        scratch_shapes=[pltpu.VMEM((span, features), BF), pltpu.SemaphoreType.DMA(())],
        compiler_params=pltpu.CompilerParams(vmem_limit_bytes=VMEM_LIMIT),
    )(target, moved, in_hbm(text))


def project_send_kernel(order_ref, rows_ref, squares_ref, *refs):
    weight_refs, out_ref = refs[:-1], refs[-1]
    width = weight_refs[0].shape[2]
    for i in range(NY):
        put_head(i, order_ref, rows_ref, weight_refs, out_ref.at[i])
        out_ref[i, width:] = squares_ref[...]


def project_send(order, rows, squares, weights):
    span = rows.shape[1]
    width = weights[0].shape[2]
    return pl.pallas_call(
        project_send_kernel,
        in_specs=[IN_SMEM] + [IN_VMEM] * (2 + len(weights)),
        out_specs=IN_VMEM,
        out_shape=jax.ShapeDtypeStruct((NY, width + 16, span), BF),
        compiler_params=pltpu.CompilerParams(vmem_limit_bytes=VMEM_LIMIT),
    )(order, rows, squares, *weights)


def pair_kernel(lines, own_ref, got_ref, *out_refs):
    rows = own_ref.shape[1] - lines
    for i, out_ref in enumerate(out_refs):
        total = own_ref[i].astype(F32) + got_ref[i].astype(F32)
        out_ref[:rows] = total[:rows].astype(BF)
        if lines:
            out_ref[rows:] = two_lines(total[rows : rows + 1] + total[rows + 1 : rows + 2])


def add_pair(lines, own, got):
    return pl.pallas_call(
        functools.partial(pair_kernel, lines),
        out_shape=[jax.ShapeDtypeStruct(own.shape[1:], BF)] * NY,
        compiler_params=pltpu.CompilerParams(vmem_limit_bytes=VMEM_LIMIT),
    )(own, got)


def finish_kernel(features, a, b, c, d, cos_ref, sin_ref, keys_ref, values_ref):
    head = keys_ref.shape[1]
    half = head // 2
    total = a[...].astype(F32)
    for part in (b, c, d):
        total = total + part[...].astype(F32)
    squares = total[2 * head : 2 * head + 1] + total[2 * head + 1 : 2 * head + 2]
    scale = lax.rsqrt(squares / features + EPS)
    lower, upper = total[:half] * scale, total[half:head] * scale
    cos, sin = cos_ref[...], sin_ref[...]
    turned = jnp.concatenate([lower * cos - upper * sin, upper * cos + lower * sin], axis=0)
    keys_ref[...] = turned.T.astype(BF)
    values_ref[...] = (total[head : 2 * head] * scale).T.astype(BF)


def finish(features, parts, cos, sin):
    half, span = cos.shape
    return pl.pallas_call(
        functools.partial(finish_kernel, features),
        out_shape=[jax.ShapeDtypeStruct((span, 2 * half), BF)] * 2,
        compiler_params=pltpu.CompilerParams(vmem_limit_bytes=VMEM_LIMIT),
    )(*parts, cos, sin)


def rotary(positions, head):
    half = head // 2
    frequency = THETA ** (-jnp.arange(half, dtype=F32) * 2.0 / head)
    angles = frequency[:, None] * positions[None, :]
    return jnp.cos(angles), jnp.sin(angles)


def body(
    patches,
    slot_page,
    page_start,
    patch_gain,
    patch_bias,
    merge_in,
    merge_out,
    text,
    norm_gain,
    kv_weight,
):
    enc_index, tp_index = lax.axis_index("enc"), lax.axis_index("tp")
    z_index, x_index = enc_index // NX, enc_index % NX
    y_index, core = tp_index // NC, tp_index % NC
    slots, page_rows, _ = patches.shape
    pages = page_start.shape[0]
    span, features = text.shape
    chunk = page_rows // NZ

    depth, wide = merge_out.shape
    scaled = (kv_weight.T.astype(F32) * norm_gain[None, :]).astype(BF)
    tails = [scaled[:, i : i + wide] for i in range(0, features, wide)]
    block = jnp.concatenate([merge_out, *tails], axis=0)
    middle = block.shape[0] // 2
    up = [block, lax.ppermute(block, "enc", shift_z(-1))]
    down = [block, lax.ppermute(block, "enc", shift_z(1))]
    hidden = hidden_rows(patches, patch_gain, patch_bias, merge_in)
    hidden, up[1], down[1] = lax.optimization_barrier((hidden, up[1], down[1]))
    for _ in range(NZ // 2 - 2):
        up.append(lax.ppermute(up[-1], "enc", shift_z(-1)))
        down.append(lax.ppermute(down[-1], "enc", shift_z(1)))

    dealt = lax.all_to_all(hidden, "enc", 0, 0, axis_index_groups=GROUPS_Z, tiled=True)
    pieces = [dealt] + [lax.ppermute(dealt, "enc", shift_x(d)) for d in range(1, NX)]
    pieces[1], up[-1], down[-1] = lax.optimization_barrier((pieces[1], up[-1], down[-1]))
    far = [
        lax.ppermute(up[-1][:middle], "enc", shift_z(-1)),
        lax.ppermute(down[-1][middle:], "enc", shift_z(1)),
    ]
    blocks = up + far + down[:0:-1]

    page_ids = jnp.arange(pages, dtype=jnp.int32)
    slot_ids = jnp.arange(slot_page.shape[0], dtype=jnp.int32)
    slot_of = jnp.sum(
        jnp.where(slot_page[None, :] == page_ids[:, None], slot_ids[None, :], 0), axis=1
    )
    holder = slot_of // slots
    place = (x_index - holder % NX) % NX * NZ + holder // NX
    place = (place * slots + slot_of % slots) * chunk
    target = (place[:, None] + jnp.arange(chunk, dtype=jnp.int32)[None, :]).reshape(-1, 1)

    live = live_rows(target, pieces)
    side = (z_index + core) % NC
    steps = jnp.arange(NY, dtype=jnp.int32) * NC

    def plan(side):
        owner = (z_index + steps + side) % NZ // NC
        return (owner - y_index) % NY

    plan = jnp.concatenate([1 - side[None], plan(1 - side), plan(side)])
    away, *kv_own, kept = send_parts(plan, live, blocks)
    got = lax.ppermute(away, "tp", SWAP_CORE)
    after = [lax.ppermute(part, "enc", shift_x(-1)) for part in kv_own]
    before = [lax.ppermute(part, "enc", shift_x(1)) for part in kv_own]
    parts = keep_parts(live, got, kept)
    others = [lax.ppermute(parts[d], "tp", shift_y(d)) for d in range(1, NY)]
    opposite = [
        lax.ppermute(after[0], "enc", shift_x(-1)),
        lax.ppermute(before[1], "enc", shift_x(1)),
    ]
    total = parts[0].astype(F32)
    for other in others:
        total = total + other.astype(F32)
    merged = total.astype(BF)
    kv_all = [*kv_own, *after, *opposite, *before]

    moved = lax.all_to_all(merged, "enc", 0, 0, tiled=True)
    per_block = pages // (NZ * NX)
    moved = moved.reshape(NZ * NX, per_block * chunk, merged.shape[1])
    starts = lax.dynamic_slice_in_dim(page_start, enc_index * per_block, per_block)
    starts = starts - enc_index * span
    rows = (
        jnp.arange(NZ, dtype=jnp.int32)[:, None, None] * chunk
        + starts[None, :, None]
        + jnp.arange(chunk, dtype=jnp.int32)[None, None, :]
    ).reshape(1, -1)
    shifted = (y_index + jnp.arange(NY, dtype=jnp.int32)) % NY * NC
    order = jnp.concatenate([shifted - z_index, (jnp.arange(NX, dtype=jnp.int32) + x_index) % NX])
    turn = jnp.arange(2 * NY, dtype=jnp.int32) < NY
    own_heads = jnp.where(turn, (order + core) % NZ, order)
    other_heads = jnp.where(turn, (order + 1 - core) % NZ, order)
    mixed, squares = mix(rows, moved, text)
    away = project_send(other_heads, mixed, squares, kv_all)
    got = lax.ppermute(away, "tp", SWAP_CORE)
    own = project_send(own_heads, mixed, squares, kv_all)
    sums = add_pair(16, own, got)
    sums = [sums[0]] + [lax.ppermute(sums[d], "tp", shift_y(d)) for d in range(1, NY)]

    positions = (enc_index * span + jnp.arange(span, dtype=jnp.int32)).astype(F32)
    cos, sin = rotary(positions, wide // 2)
    return tuple(finish(features * NY * NC, sums, cos, sin))


def solution(mesh):
    return jax.shard_map(
        body,
        mesh=mesh,
        in_specs=(
            P(("rep", "enc"), None, None),
            P("rep"),
            P("rep"),
            P(),
            P(),
            P(None, "tp"),
            P("tp", "enc"),
            P(("rep", "enc"), "tp"),
            P("tp"),
            P("tp", "enc"),
        ),
        out_specs=(P(("rep", "enc"), "tp"), P(("rep", "enc"), "tp")),
        check_vma=False,
    )
```

```python
import functools

import jax
import jax.numpy as jnp
from jax import lax
from jax.experimental import pallas as pl
from jax.experimental.pallas import tpu as pltpu
from jax.sharding import PartitionSpec as P

EPS = 1e-06
THETA = 1000000.0
NZ, NX, NY, NC = 8, 4, 4, 2
VMEM_LIMIT = 24 * 1024 * 1024
BF = jnp.bfloat16
F32 = jnp.float32

FAR_FIRST, FAR_LAST = (2, 1, 3), (3, 1, 2)
GROUPS_Z = [[z * NX + x for z in range(NZ)] for x in range(NX)]


def shift_x(d):
    return [(z * NX + x, z * NX + (x + d) % NX) for z in range(NZ) for x in range(NX)]


def shift_z(d):
    return [(z * NX + x, (z + d) % NZ * NX + x) for z in range(NZ) for x in range(NX)]


def shift_y(d):
    return [(y * NC + c, (y + d) % NY * NC + c) for y in range(NY) for c in range(NC)]


SWAP_CORE = [(t, t ^ 1) for t in range(NY * NC)]


IN_VMEM = pl.BlockSpec(memory_space=pltpu.VMEM)
IN_SMEM = pl.BlockSpec(memory_space=pltpu.SMEM)
IN_HBM = pl.BlockSpec(memory_space=pltpu.HBM)


def in_hbm(array):
    return pltpu.with_memory_space_constraint(array, pltpu.HBM)


def hidden_kernel(
    slots,
    patch_ref,
    gain_ref,
    bias_ref,
    weight_ref,
    out_ref,
    patch_buf,
    weight_buf,
    gain_buf,
    bias_buf,
    sems,
):
    width = weight_buf.shape[1]
    groups = weight_buf.shape[0]
    small = (
        pltpu.make_async_copy(gain_ref, gain_buf, sems.at[0, groups]),
        pltpu.make_async_copy(bias_ref, bias_buf, sems.at[1, groups]),
    )
    for copy in small:
        copy.start()
    copies = []
    for i in range(groups):
        part = pl.ds(i * width, width)
        pair = (
            pltpu.make_async_copy(patch_ref.at[:, part], patch_buf.at[i], sems.at[0, i]),
            pltpu.make_async_copy(weight_ref.at[part], weight_buf.at[i], sems.at[1, i]),
        )
        for copy in pair:
            copy.start()
        copies.append(pair)
    for copy in small:
        copy.wait()
    gain, bias = gain_buf[...][None, :], bias_buf[...][None, :]
    total = None
    for i, pair in enumerate(copies):
        pair[0].wait()
        part = patch_buf[i].astype(F32)
        center = jnp.mean(part, axis=-1, keepdims=True)
        part = part - center
        spread = jnp.mean(part * part, axis=-1, keepdims=True)
        normed = (part * lax.rsqrt(spread + EPS) * gain + bias).astype(BF)
        pair[1].wait()
        term = jnp.dot(normed, weight_buf[i], preferred_element_type=F32)
        total = term if total is None else total + term
    total = 0.5 * total * (1.0 + lax.erf(total * 0.7071067811865476))
    rows = total.shape[0] // slots
    chunk = rows // NZ
    pieces = [
        total[slot * rows + z * chunk : slot * rows + (z + 1) * chunk]
        for z in range(NZ)
        for slot in range(slots)
    ]
    out_ref[...] = jnp.concatenate(pieces, axis=0).astype(BF)


def hidden_rows(patches, patch_gain, patch_bias, merge_in):
    slots, rows, feature = patches.shape
    width = patch_gain.shape[0]
    groups = feature // width
    flat = patches.reshape(slots * rows, feature)
    out_width = merge_in.shape[1]
    return pl.pallas_call(
        functools.partial(hidden_kernel, slots),
        in_specs=[IN_HBM] * 4,
        out_specs=IN_VMEM,
        out_shape=jax.ShapeDtypeStruct((slots * rows, out_width), BF),
        scratch_shapes=[
            pltpu.VMEM((groups, slots * rows, width), BF),
            pltpu.VMEM((groups, width, out_width), BF),
            pltpu.VMEM((width,), F32),
            pltpu.VMEM((width,), F32),
            pltpu.SemaphoreType.DMA((2, groups + 1)),
        ],
        compiler_params=pltpu.CompilerParams(vmem_limit_bytes=VMEM_LIMIT),
    )(in_hbm(flat), in_hbm(patch_gain), in_hbm(patch_bias), in_hbm(merge_in))


def live_kernel(target_ref, a, b, c, d, live_ref):
    target = target_ref[...]
    total = None
    for index, piece in enumerate((a, b, c, d)):
        rows = piece.shape[0]
        place = lax.broadcasted_iota(jnp.int32, (target.shape[0], rows), 1) + index * rows
        pick = jnp.where(place == target, 1.0, 0.0).astype(BF)
        term = jnp.dot(pick, piece[...], preferred_element_type=F32)
        total = term if total is None else total + term
    live_ref[...] = total.astype(BF)


def live_rows(target, pieces):
    rows, depth = target.shape[0], pieces[0].shape[1]
    return pl.pallas_call(
        live_kernel,
        out_shape=jax.ShapeDtypeStruct((rows, depth), BF),
        compiler_params=pltpu.CompilerParams(vmem_limit_bytes=VMEM_LIMIT),
    )(target, *pieces)


def fetch_rows(blocks, r, start, rows, target, sems):
    if r == NZ // 2:
        cut = blocks[r].shape[0]
        spans = []
        if start < cut:
            spans.append((blocks[r], start, 0, min(rows, cut - start)))
        if start + rows > cut:
            skip = max(cut - start, 0)
            spans.append((blocks[r + 1], start + skip - cut, skip, rows - skip))
    else:
        spans = [(blocks[r if r < NZ // 2 else r + 1], start, 0, rows)]
    copies = [
        pltpu.make_async_copy(
            ref.at[pl.ds(at, count)], target.at[pl.ds(to, count)], sems.at[index]
        )
        for index, (ref, at, to, count) in enumerate(spans)
    ]
    for copy in copies:
        copy.start()
    return copies


def send_kernel(plan_ref, live_ref, *refs):
    depth = live_ref.shape[1]
    blocks, (out_ref, low_ref, high_ref, kept_ref, buf, sems, kv_sems, kept_sems) = (
        refs[:-8],
        refs[-8:],
    )
    half = low_ref.shape[1]
    copies = []
    for r in range(NZ):
        copies += fetch_rows(blocks, r, depth, half, low_ref.at[r], kv_sems.at[0, r])
        copies += fetch_rows(blocks, r, depth + half, half, high_ref.at[r], kv_sems.at[1, r])
    for side in range(NC):

        @pl.when(plan_ref[0] == side)
        def _(side=side):
            groups = [
                fetch_rows(blocks, NC * j + side, 0, depth, buf.at[j], sems.at[j])
                for j in range(NY)
            ]
            kept = []
            for j in range(NY):
                target = kept_ref.at[plan_ref[1 + NY + j]]
                kept += fetch_rows(
                    blocks, NC * j + 1 - side, 0, depth, target, kept_sems.at[j]
                )
            for j, group in enumerate(groups):
                for copy in group:
                    copy.wait()
                part = jnp.dot(live_ref[...], buf[j], preferred_element_type=F32)
                out_ref[plan_ref[1 + j]] = part.astype(BF)
            for copy in kept:
                copy.wait()

    for copy in copies:
        copy.wait()


def send_parts(plan, live, blocks):
    rows, depth = live.shape
    width = blocks[0].shape[1]
    half = (blocks[0].shape[0] - depth) // 2
    return pl.pallas_call(
        send_kernel,
        in_specs=[IN_SMEM, IN_VMEM] + [IN_HBM] * len(blocks),
        out_specs=[IN_VMEM, IN_HBM, IN_HBM, IN_VMEM],
        out_shape=[jax.ShapeDtypeStruct((NY, rows, width), BF)]
        + [jax.ShapeDtypeStruct((NZ, half, width), BF)] * 2
        + [jax.ShapeDtypeStruct((NY, depth, width), BF)],
        scratch_shapes=[
            pltpu.VMEM((NY, depth, width), BF),
            pltpu.SemaphoreType.DMA((NY, 2)),
            pltpu.SemaphoreType.DMA((2, NZ, 2)),
            pltpu.SemaphoreType.DMA((NY, 2)),
        ],
        compiler_params=pltpu.CompilerParams(vmem_limit_bytes=VMEM_LIMIT),
    )(plan, live, *[in_hbm(block) for block in blocks])


def keep_kernel(live_ref, got_ref, weight_ref, *out_refs):
    for d, out_ref in enumerate(out_refs):
        own = jnp.dot(live_ref[...], weight_ref[d], preferred_element_type=F32).astype(BF)
        out_ref[...] = (own.astype(F32) + got_ref[d].astype(F32)).astype(BF)


def keep_parts(live, got, weights):
    rows, width = live.shape[0], weights.shape[2]
    return pl.pallas_call(
        keep_kernel,
        out_shape=[jax.ShapeDtypeStruct((rows, width), BF)] * NY,
        compiler_params=pltpu.CompilerParams(vmem_limit_bytes=VMEM_LIMIT),
    )(live, got, weights)


def put_head(i, order_ref, rows_ref, weight_refs, out_ref):
    head = order_ref[i]
    rows = weight_refs[0].shape[2] // NX
    lines = []
    for d in range(NX):
        line = [
            ref[head, j * rows : (j + 1) * rows]
            for ref in weight_refs[2 * d : 2 * d + 2]
            for j in range(ref.shape[1] // rows)
        ]
        lines.append(jnp.concatenate(line, axis=1))
    part = jnp.dot(
        jnp.concatenate(lines, axis=0), rows_ref[...], preferred_element_type=F32
    ).astype(BF)
    for d in range(NX):
        place = pl.ds(pl.multiple_of(order_ref[NY + d] * rows, rows), rows)
        out_ref[place] = part[d * rows : (d + 1) * rows]


def two_lines(squares):
    squares = jnp.broadcast_to(squares, (16, squares.shape[1]))
    high = squares.astype(BF).astype(F32)
    line = lax.broadcasted_iota(jnp.int32, squares.shape, 0)
    return jnp.where(line == 0, high, jnp.where(line == 1, squares - high, 0.0)).astype(BF)


def mix_kernel(target_ref, moved_ref, text_ref, rows_ref, squares_ref, text_buf, sem):
    text_copy = pltpu.make_async_copy(text_ref, text_buf, sem)
    text_copy.start()
    span = text_ref.shape[0]
    target = target_ref[...]
    place = lax.broadcasted_iota(jnp.int32, (span, target.shape[1]), 0) == target
    pick = jnp.where(place, 1.0, 0.0)
    covered = jnp.sum(pick, axis=1, keepdims=True) > 0.5
    pick = pick.astype(BF)
    width = moved_ref.shape[2]
    squares = jnp.zeros((1, span), F32)
    text_copy.wait()
    for x in range(NX):
        stacked = jnp.concatenate([moved_ref[z * NX + x] for z in range(NZ)], axis=0)
        put = jnp.dot(pick, stacked, preferred_element_type=F32)
        columns = slice(x * width, (x + 1) * width)
        mixed = jnp.where(covered, put, text_buf[:, columns].astype(F32)).T
        rows_ref[columns] = mixed.astype(BF)
        squares += jnp.sum(mixed * mixed, axis=0, keepdims=True)
    squares_ref[...] = two_lines(squares)


def mix(target, moved, text):
    span, features = text.shape
    return pl.pallas_call(
        mix_kernel,
        in_specs=[IN_VMEM, IN_VMEM, IN_HBM],
        out_specs=[IN_VMEM] * 2,
        out_shape=[
            jax.ShapeDtypeStruct((features, span), BF),
            jax.ShapeDtypeStruct((16, span), BF),
        ],
        scratch_shapes=[pltpu.VMEM((span, features), BF), pltpu.SemaphoreType.DMA(())],
        compiler_params=pltpu.CompilerParams(vmem_limit_bytes=VMEM_LIMIT),
    )(target, moved, in_hbm(text))


def project_send_kernel(order_ref, rows_ref, squares_ref, *refs):
    weight_refs, out_ref = refs[:-1], refs[-1]
    width = weight_refs[0].shape[2]
    for i in range(NY):
        put_head(i, order_ref, rows_ref, weight_refs, out_ref.at[i])
        out_ref[i, width:] = squares_ref[...]


def project_send(order, rows, squares, weights):
    span = rows.shape[1]
    width = weights[0].shape[2]
    return pl.pallas_call(
        project_send_kernel,
        in_specs=[IN_SMEM] + [IN_VMEM] * (2 + len(weights)),
        out_specs=IN_VMEM,
        out_shape=jax.ShapeDtypeStruct((NY, width + 16, span), BF),
        compiler_params=pltpu.CompilerParams(vmem_limit_bytes=VMEM_LIMIT),
    )(order, rows, squares, *weights)


def pair_kernel(lines, own_ref, got_ref, *out_refs):
    rows = own_ref.shape[1] - lines
    for i, out_ref in enumerate(out_refs):
        total = own_ref[i].astype(F32) + got_ref[i].astype(F32)
        out_ref[:rows] = total[:rows].astype(BF)
        if lines:
            out_ref[rows:] = two_lines(total[rows : rows + 1] + total[rows + 1 : rows + 2])


def add_pair(lines, own, got):
    return pl.pallas_call(
        functools.partial(pair_kernel, lines),
        out_shape=[jax.ShapeDtypeStruct(own.shape[1:], BF)] * NY,
        compiler_params=pltpu.CompilerParams(vmem_limit_bytes=VMEM_LIMIT),
    )(own, got)


def finish_kernel(features, a, b, c, d, cos_ref, sin_ref, keys_ref, values_ref):
    head = keys_ref.shape[1]
    half = head // 2
    total = a[...].astype(F32)
    for part in (b, c, d):
        total = total + part[...].astype(F32)
    squares = total[2 * head : 2 * head + 1] + total[2 * head + 1 : 2 * head + 2]
    scale = lax.rsqrt(squares / features + EPS)
    lower, upper = total[:half] * scale, total[half:head] * scale
    cos, sin = cos_ref[...], sin_ref[...]
    turned = jnp.concatenate([lower * cos - upper * sin, upper * cos + lower * sin], axis=0)
    keys_ref[...] = turned.T.astype(BF)
    values_ref[...] = (total[head : 2 * head] * scale).T.astype(BF)


def finish(features, parts, cos, sin):
    half, span = cos.shape
    return pl.pallas_call(
        functools.partial(finish_kernel, features),
        out_shape=[jax.ShapeDtypeStruct((span, 2 * half), BF)] * 2,
        compiler_params=pltpu.CompilerParams(vmem_limit_bytes=VMEM_LIMIT),
    )(*parts, cos, sin)


def rotary(positions, head):
    half = head // 2
    frequency = THETA ** (-jnp.arange(half, dtype=F32) * 2.0 / head)
    angles = frequency[:, None] * positions[None, :]
    return jnp.cos(angles), jnp.sin(angles)


def body(
    patches,
    slot_page,
    page_start,
    patch_gain,
    patch_bias,
    merge_in,
    merge_out,
    text,
    norm_gain,
    kv_weight,
):
    enc_index, tp_index = lax.axis_index("enc"), lax.axis_index("tp")
    z_index, x_index = enc_index // NX, enc_index % NX
    y_index, core = tp_index // NC, tp_index % NC
    slots, page_rows, _ = patches.shape
    pages = page_start.shape[0]
    span, features = text.shape
    chunk = page_rows // NZ

    depth, wide = merge_out.shape
    scaled = (kv_weight.T.astype(F32) * norm_gain[None, :]).astype(BF)
    tails = [scaled[:, i : i + wide] for i in range(0, features, wide)]
    block = jnp.concatenate([merge_out, *tails], axis=0)
    middle = block.shape[0] // 2
    up = [block, lax.ppermute(block, "enc", shift_z(-1))]
    down = [block, lax.ppermute(block, "enc", shift_z(1))]
    hidden = hidden_rows(patches, patch_gain, patch_bias, merge_in)
    hidden, up[1], down[1] = lax.optimization_barrier((hidden, up[1], down[1]))
    for _ in range(NZ // 2 - 2):
        up.append(lax.ppermute(up[-1], "enc", shift_z(-1)))
        down.append(lax.ppermute(down[-1], "enc", shift_z(1)))

    dealt = lax.all_to_all(hidden, "enc", 0, 0, axis_index_groups=GROUPS_Z, tiled=True)
    pieces = [dealt] + [lax.ppermute(dealt, "enc", shift_x(d)) for d in range(1, NX)]
    pieces[1], up[-1], down[-1] = lax.optimization_barrier((pieces[1], up[-1], down[-1]))
    far = [
        lax.ppermute(up[-1][:middle], "enc", shift_z(-1)),
        lax.ppermute(down[-1][middle:], "enc", shift_z(1)),
    ]
    blocks = up + far + down[:0:-1]

    page_ids = jnp.arange(pages, dtype=jnp.int32)
    slot_ids = jnp.arange(slot_page.shape[0], dtype=jnp.int32)
    slot_of = jnp.sum(
        jnp.where(slot_page[None, :] == page_ids[:, None], slot_ids[None, :], 0), axis=1
    )
    holder = slot_of // slots
    place = (x_index - holder % NX) % NX * NZ + holder // NX
    place = (place * slots + slot_of % slots) * chunk
    target = (place[:, None] + jnp.arange(chunk, dtype=jnp.int32)[None, :]).reshape(-1, 1)

    live = live_rows(target, pieces)
    side = (z_index + core) % NC
    steps = jnp.arange(NY, dtype=jnp.int32) * NC

    def plan(side):
        owner = (z_index + steps + side) % NZ // NC
        return (owner - y_index) % NY

    plan = jnp.concatenate([1 - side[None], plan(1 - side), plan(side)])
    away, *kv_own, kept = send_parts(plan, live, blocks)
    got = lax.ppermute(away, "tp", SWAP_CORE)
    after = [lax.ppermute(part, "enc", shift_x(-1)) for part in kv_own]
    before = [lax.ppermute(part, "enc", shift_x(1)) for part in kv_own]
    parts = keep_parts(live, got, kept)
    others = [lax.ppermute(parts[d], "tp", shift_y(d)) for d in FAR_LAST]
    opposite = [
        lax.ppermute(after[0], "enc", shift_x(-1)),
        lax.ppermute(before[1], "enc", shift_x(1)),
    ]
    total = parts[0].astype(F32)
    for other in others:
        total = total + other.astype(F32)
    merged = total.astype(BF)
    kv_all = [*kv_own, *after, *opposite, *before]

    moved = lax.all_to_all(merged, "enc", 0, 0, tiled=True)
    per_block = pages // (NZ * NX)
    moved = moved.reshape(NZ * NX, per_block * chunk, merged.shape[1])
    starts = lax.dynamic_slice_in_dim(page_start, enc_index * per_block, per_block)
    starts = starts - enc_index * span
    rows = (
        jnp.arange(NZ, dtype=jnp.int32)[:, None, None] * chunk
        + starts[None, :, None]
        + jnp.arange(chunk, dtype=jnp.int32)[None, None, :]
    ).reshape(1, -1)
    shifted = (y_index + jnp.arange(NY, dtype=jnp.int32)) % NY * NC
    order = jnp.concatenate([shifted - z_index, (jnp.arange(NX, dtype=jnp.int32) + x_index) % NX])
    turn = jnp.arange(2 * NY, dtype=jnp.int32) < NY
    own_heads = jnp.where(turn, (order + core) % NZ, order)
    other_heads = jnp.where(turn, (order + 1 - core) % NZ, order)
    mixed, squares = mix(rows, moved, text)
    away = project_send(other_heads, mixed, squares, kv_all)
    got = lax.ppermute(away, "tp", SWAP_CORE)
    own = project_send(own_heads, mixed, squares, kv_all)
    sums = add_pair(16, own, got)
    sums = [sums[0]] + [lax.ppermute(sums[d], "tp", shift_y(d)) for d in FAR_FIRST]

    positions = (enc_index * span + jnp.arange(span, dtype=jnp.int32)).astype(F32)
    cos, sin = rotary(positions, wide // 2)
    return tuple(finish(features * NY * NC, sums, cos, sin))


def solution(mesh):
    return jax.shard_map(
        body,
        mesh=mesh,
        in_specs=(
            P(("rep", "enc"), None, None),
            P("rep"),
            P("rep"),
            P(),
            P(),
            P(None, "tp"),
            P("tp", "enc"),
            P(("rep", "enc"), "tp"),
            P("tp"),
            P("tp", "enc"),
        ),
        out_specs=(P(("rep", "enc"), "tp"), P(("rep", "enc"), "tp")),
        check_vma=False,
    )
```

```python
import functools

import jax
import jax.numpy as jnp
from jax import lax
from jax.experimental import pallas as pl
from jax.experimental.pallas import tpu as pltpu
from jax.sharding import PartitionSpec as P

EPS = 1e-06
THETA = 1000000.0
NZ, NX, NY, NC = 8, 4, 4, 2
VMEM_LIMIT = 24 * 1024 * 1024
BF = jnp.bfloat16
F32 = jnp.float32

FAR_FIRST, FAR_LAST = (2, 1, 3), (3, 1, 2)
GROUPS_Z = [[z * NX + x for z in range(NZ)] for x in range(NX)]


def shift_x(d):
    return [(z * NX + x, z * NX + (x + d) % NX) for z in range(NZ) for x in range(NX)]


def shift_z(d):
    return [(z * NX + x, (z + d) % NZ * NX + x) for z in range(NZ) for x in range(NX)]


def shift_y(d):
    return [(y * NC + c, (y + d) % NY * NC + c) for y in range(NY) for c in range(NC)]


SWAP_CORE = [(t, t ^ 1) for t in range(NY * NC)]


IN_VMEM = pl.BlockSpec(memory_space=pltpu.VMEM)
IN_SMEM = pl.BlockSpec(memory_space=pltpu.SMEM)
IN_HBM = pl.BlockSpec(memory_space=pltpu.HBM)


def in_hbm(array):
    return pltpu.with_memory_space_constraint(array, pltpu.HBM)


def hidden_kernel(
    slots,
    patch_ref,
    gain_ref,
    bias_ref,
    weight_ref,
    out_ref,
    patch_buf,
    weight_buf,
    gain_buf,
    bias_buf,
    sems,
):
    width = weight_buf.shape[1]
    groups = weight_buf.shape[0]
    small = (
        pltpu.make_async_copy(gain_ref, gain_buf, sems.at[0, groups]),
        pltpu.make_async_copy(bias_ref, bias_buf, sems.at[1, groups]),
    )
    for copy in small:
        copy.start()
    copies = []
    for i in range(groups):
        part = pl.ds(i * width, width)
        pair = (
            pltpu.make_async_copy(patch_ref.at[:, part], patch_buf.at[i], sems.at[0, i]),
            pltpu.make_async_copy(weight_ref.at[part], weight_buf.at[i], sems.at[1, i]),
        )
        for copy in pair:
            copy.start()
        copies.append(pair)
    for copy in small:
        copy.wait()
    gain, bias = gain_buf[...][None, :], bias_buf[...][None, :]
    total = None
    for i, pair in enumerate(copies):
        pair[0].wait()
        part = patch_buf[i].astype(F32)
        center = jnp.mean(part, axis=-1, keepdims=True)
        part = part - center
        spread = jnp.mean(part * part, axis=-1, keepdims=True)
        normed = (part * lax.rsqrt(spread + EPS) * gain + bias).astype(BF)
        pair[1].wait()
        term = jnp.dot(normed, weight_buf[i], preferred_element_type=F32)
        total = term if total is None else total + term
    total = 0.5 * total * (1.0 + lax.erf(total * 0.7071067811865476))
    rows = total.shape[0] // slots
    chunk = rows // NZ
    pieces = [
        total[slot * rows + z * chunk : slot * rows + (z + 1) * chunk]
        for z in range(NZ)
        for slot in range(slots)
    ]
    out_ref[...] = jnp.concatenate(pieces, axis=0).astype(BF)


def hidden_rows(patches, patch_gain, patch_bias, merge_in):
    slots, rows, feature = patches.shape
    width = patch_gain.shape[0]
    groups = feature // width
    flat = patches.reshape(slots * rows, feature)
    out_width = merge_in.shape[1]
    return pl.pallas_call(
        functools.partial(hidden_kernel, slots),
        in_specs=[IN_HBM] * 4,
        out_specs=IN_VMEM,
        out_shape=jax.ShapeDtypeStruct((slots * rows, out_width), BF),
        scratch_shapes=[
            pltpu.VMEM((groups, slots * rows, width), BF),
            pltpu.VMEM((groups, width, out_width), BF),
            pltpu.VMEM((width,), F32),
            pltpu.VMEM((width,), F32),
            pltpu.SemaphoreType.DMA((2, groups + 1)),
        ],
        compiler_params=pltpu.CompilerParams(vmem_limit_bytes=VMEM_LIMIT),
    )(in_hbm(flat), in_hbm(patch_gain), in_hbm(patch_bias), in_hbm(merge_in))


def live_kernel(target_ref, a, b, c, d, live_ref):
    target = target_ref[...]
    total = None
    for index, piece in enumerate((a, b, c, d)):
        rows = piece.shape[0]
        place = lax.broadcasted_iota(jnp.int32, (target.shape[0], rows), 1) + index * rows
        pick = jnp.where(place == target, 1.0, 0.0).astype(BF)
        term = jnp.dot(pick, piece[...], preferred_element_type=F32)
        total = term if total is None else total + term
    live_ref[...] = total.astype(BF)


def live_rows(target, pieces):
    rows, depth = target.shape[0], pieces[0].shape[1]
    return pl.pallas_call(
        live_kernel,
        out_shape=jax.ShapeDtypeStruct((rows, depth), BF),
        compiler_params=pltpu.CompilerParams(vmem_limit_bytes=VMEM_LIMIT),
    )(target, *pieces)


def fetch_rows(blocks, r, start, rows, target, sems):
    if r == NZ // 2:
        cut = blocks[r].shape[0]
        spans = []
        if start < cut:
            spans.append((blocks[r], start, 0, min(rows, cut - start)))
        if start + rows > cut:
            skip = max(cut - start, 0)
            spans.append((blocks[r + 1], start + skip - cut, skip, rows - skip))
    else:
        spans = [(blocks[r if r < NZ // 2 else r + 1], start, 0, rows)]
    copies = [
        pltpu.make_async_copy(
            ref.at[pl.ds(at, count)], target.at[pl.ds(to, count)], sems.at[index]
        )
        for index, (ref, at, to, count) in enumerate(spans)
    ]
    for copy in copies:
        copy.start()
    return copies


def send_kernel(plan_ref, live_ref, *refs):
    depth = live_ref.shape[1]
    blocks, (out_ref, low_ref, high_ref, kept_ref, buf, sems, kv_sems, kept_sems) = (
        refs[:-8],
        refs[-8:],
    )
    half = low_ref.shape[1]
    copies = []
    for r in range(NZ):
        copies += fetch_rows(blocks, r, depth, half, low_ref.at[r], kv_sems.at[0, r])
        copies += fetch_rows(blocks, r, depth + half, half, high_ref.at[r], kv_sems.at[1, r])
    for side in range(NC):

        @pl.when(plan_ref[0] == side)
        def _(side=side):
            groups = [
                fetch_rows(blocks, NC * j + side, 0, depth, buf.at[j], sems.at[j])
                for j in range(NY)
            ]
            kept = []
            for j in range(NY):
                target = kept_ref.at[plan_ref[1 + NY + j]]
                kept += fetch_rows(
                    blocks, NC * j + 1 - side, 0, depth, target, kept_sems.at[j]
                )
            for j, group in enumerate(groups):
                for copy in group:
                    copy.wait()
                part = jnp.dot(live_ref[...], buf[j], preferred_element_type=F32)
                out_ref[plan_ref[1 + j]] = part.astype(BF)
            for copy in kept:
                copy.wait()

    for copy in copies:
        copy.wait()


def send_parts(plan, live, blocks):
    rows, depth = live.shape
    width = blocks[0].shape[1]
    half = (blocks[0].shape[0] - depth) // 2
    return pl.pallas_call(
        send_kernel,
        in_specs=[IN_SMEM, IN_VMEM] + [IN_HBM] * len(blocks),
        out_specs=[IN_VMEM, IN_HBM, IN_HBM, IN_VMEM],
        out_shape=[jax.ShapeDtypeStruct((NY, rows, width), BF)]
        + [jax.ShapeDtypeStruct((NZ, half, width), BF)] * 2
        + [jax.ShapeDtypeStruct((NY, depth, width), BF)],
        scratch_shapes=[
            pltpu.VMEM((NY, depth, width), BF),
            pltpu.SemaphoreType.DMA((NY, 2)),
            pltpu.SemaphoreType.DMA((2, NZ, 2)),
            pltpu.SemaphoreType.DMA((NY, 2)),
        ],
        compiler_params=pltpu.CompilerParams(vmem_limit_bytes=VMEM_LIMIT),
    )(plan, live, *[in_hbm(block) for block in blocks])


def keep_kernel(live_ref, got_ref, weight_ref, *out_refs):
    for d, out_ref in enumerate(out_refs):
        own = jnp.dot(live_ref[...], weight_ref[d], preferred_element_type=F32).astype(BF)
        out_ref[...] = (own.astype(F32) + got_ref[d].astype(F32)).astype(BF)


def keep_parts(live, got, weights):
    rows, width = live.shape[0], weights.shape[2]
    return pl.pallas_call(
        keep_kernel,
        out_shape=[jax.ShapeDtypeStruct((rows, width), BF)] * NY,
        compiler_params=pltpu.CompilerParams(vmem_limit_bytes=VMEM_LIMIT),
    )(live, got, weights)


def put_head(i, order_ref, rows_ref, weight_refs, out_ref):
    head = order_ref[i]
    rows = weight_refs[0].shape[2] // NX
    lines = []
    for d in range(NX):
        line = [
            ref[head, j * rows : (j + 1) * rows]
            for ref in weight_refs[2 * d : 2 * d + 2]
            for j in range(ref.shape[1] // rows)
        ]
        lines.append(jnp.concatenate(line, axis=1))
    part = jnp.dot(
        jnp.concatenate(lines, axis=0), rows_ref[...], preferred_element_type=F32
    ).astype(BF)
    for d in range(NX):
        place = pl.ds(pl.multiple_of(order_ref[NY + d] * rows, rows), rows)
        out_ref[place] = part[d * rows : (d + 1) * rows]


def two_lines(squares):
    squares = jnp.broadcast_to(squares, (16, squares.shape[1]))
    high = squares.astype(BF).astype(F32)
    line = lax.broadcasted_iota(jnp.int32, squares.shape, 0)
    return jnp.where(line == 0, high, jnp.where(line == 1, squares - high, 0.0)).astype(BF)


def mix_kernel(target_ref, moved_ref, text_ref, rows_ref, squares_ref, text_buf, sem):
    text_copy = pltpu.make_async_copy(text_ref, text_buf, sem)
    text_copy.start()
    span = text_ref.shape[0]
    target = target_ref[...]
    place = lax.broadcasted_iota(jnp.int32, (span, target.shape[1]), 0) == target
    pick = jnp.where(place, 1.0, 0.0)
    covered = jnp.sum(pick, axis=1, keepdims=True) > 0.5
    pick = pick.astype(BF)
    width = moved_ref.shape[2]
    squares = jnp.zeros((1, span), F32)
    text_copy.wait()
    for x in range(NX):
        stacked = jnp.concatenate([moved_ref[z * NX + x] for z in range(NZ)], axis=0)
        put = jnp.dot(pick, stacked, preferred_element_type=F32)
        columns = slice(x * width, (x + 1) * width)
        mixed = jnp.where(covered, put, text_buf[:, columns].astype(F32)).T
        rows_ref[columns] = mixed.astype(BF)
        squares += jnp.sum(mixed * mixed, axis=0, keepdims=True)
    squares_ref[...] = two_lines(squares)


def mix(target, moved, text):
    span, features = text.shape
    return pl.pallas_call(
        mix_kernel,
        in_specs=[IN_VMEM, IN_VMEM, IN_HBM],
        out_specs=[IN_VMEM] * 2,
        out_shape=[
            jax.ShapeDtypeStruct((features, span), BF),
            jax.ShapeDtypeStruct((16, span), BF),
        ],
        scratch_shapes=[pltpu.VMEM((span, features), BF), pltpu.SemaphoreType.DMA(())],
        compiler_params=pltpu.CompilerParams(vmem_limit_bytes=VMEM_LIMIT),
    )(target, moved, in_hbm(text))


def project_send_kernel(order_ref, rows_ref, squares_ref, *refs):
    weight_refs, out_ref = refs[:-1], refs[-1]
    width = weight_refs[0].shape[2]
    for i in range(NY):
        put_head(i, order_ref, rows_ref, weight_refs, out_ref.at[i])
        out_ref[i, width:] = squares_ref[...]


def project_send(order, rows, squares, weights):
    span = rows.shape[1]
    width = weights[0].shape[2]
    return pl.pallas_call(
        project_send_kernel,
        in_specs=[IN_SMEM] + [IN_VMEM] * (2 + len(weights)),
        out_specs=IN_VMEM,
        out_shape=jax.ShapeDtypeStruct((NY, width + 16, span), BF),
        compiler_params=pltpu.CompilerParams(vmem_limit_bytes=VMEM_LIMIT),
    )(order, rows, squares, *weights)


def pair_kernel(lines, own_ref, got_ref, *out_refs):
    rows = own_ref.shape[1] - lines
    for i, out_ref in enumerate(out_refs):
        total = own_ref[i].astype(F32) + got_ref[i].astype(F32)
        out_ref[:rows] = total[:rows].astype(BF)
        if lines:
            out_ref[rows:] = two_lines(total[rows : rows + 1] + total[rows + 1 : rows + 2])


def add_pair(lines, own, got):
    return pl.pallas_call(
        functools.partial(pair_kernel, lines),
        out_shape=[jax.ShapeDtypeStruct(own.shape[1:], BF)] * NY,
        compiler_params=pltpu.CompilerParams(vmem_limit_bytes=VMEM_LIMIT),
    )(own, got)


def finish_kernel(features, a, b, c, d, cos_ref, sin_ref, keys_ref, values_ref):
    head = keys_ref.shape[1]
    half = head // 2
    total = a[...].astype(F32)
    for part in (b, c, d):
        total = total + part[...].astype(F32)
    squares = total[2 * head : 2 * head + 1] + total[2 * head + 1 : 2 * head + 2]
    scale = lax.rsqrt(squares / features + EPS)
    lower, upper = total[:half] * scale, total[half:head] * scale
    cos, sin = cos_ref[...], sin_ref[...]
    turned = jnp.concatenate([lower * cos - upper * sin, upper * cos + lower * sin], axis=0)
    keys_ref[...] = turned.T.astype(BF)
    values_ref[...] = (total[head : 2 * head] * scale).T.astype(BF)


def finish(features, parts, cos, sin):
    half, span = cos.shape
    return pl.pallas_call(
        functools.partial(finish_kernel, features),
        out_shape=[jax.ShapeDtypeStruct((span, 2 * half), BF)] * 2,
        compiler_params=pltpu.CompilerParams(vmem_limit_bytes=VMEM_LIMIT),
    )(*parts, cos, sin)


def rotary(positions, head):
    half = head // 2
    frequency = THETA ** (-jnp.arange(half, dtype=F32) * 2.0 / head)
    angles = frequency[:, None] * positions[None, :]
    return jnp.cos(angles), jnp.sin(angles)


def body(
    patches,
    slot_page,
    page_start,
    patch_gain,
    patch_bias,
    merge_in,
    merge_out,
    text,
    norm_gain,
    kv_weight,
):
    enc_index, tp_index = lax.axis_index("enc"), lax.axis_index("tp")
    z_index, x_index = enc_index // NX, enc_index % NX
    y_index, core = tp_index // NC, tp_index % NC
    slots, page_rows, _ = patches.shape
    pages = page_start.shape[0]
    span, features = text.shape
    chunk = page_rows // NZ

    depth, wide = merge_out.shape
    scaled = (kv_weight.T.astype(F32) * norm_gain[None, :]).astype(BF)
    tails = [scaled[:, i : i + wide] for i in range(0, features, wide)]
    block = jnp.concatenate([merge_out, *tails], axis=0)
    middle = block.shape[0] // 2
    up = [block, lax.ppermute(block, "enc", shift_z(-1))]
    down = [block, lax.ppermute(block, "enc", shift_z(1))]
    hidden = hidden_rows(patches, patch_gain, patch_bias, merge_in)
    hidden, up[1], down[1] = lax.optimization_barrier((hidden, up[1], down[1]))
    for _ in range(NZ // 2 - 2):
        up.append(lax.ppermute(up[-1], "enc", shift_z(-1)))
        down.append(lax.ppermute(down[-1], "enc", shift_z(1)))

    dealt = lax.all_to_all(hidden, "enc", 0, 0, axis_index_groups=GROUPS_Z, tiled=True)
    by_x = {d: lax.ppermute(dealt, "enc", shift_x(d)) for d in FAR_FIRST}
    pieces = [dealt] + [by_x[d] for d in range(1, NX)]
    pieces[2], up[-1], down[-1] = lax.optimization_barrier((pieces[2], up[-1], down[-1]))
    far = [
        lax.ppermute(up[-1][:middle], "enc", shift_z(-1)),
        lax.ppermute(down[-1][middle:], "enc", shift_z(1)),
    ]
    blocks = up + far + down[:0:-1]

    page_ids = jnp.arange(pages, dtype=jnp.int32)
    slot_ids = jnp.arange(slot_page.shape[0], dtype=jnp.int32)
    slot_of = jnp.sum(
        jnp.where(slot_page[None, :] == page_ids[:, None], slot_ids[None, :], 0), axis=1
    )
    holder = slot_of // slots
    place = (x_index - holder % NX) % NX * NZ + holder // NX
    place = (place * slots + slot_of % slots) * chunk
    target = (place[:, None] + jnp.arange(chunk, dtype=jnp.int32)[None, :]).reshape(-1, 1)

    live = live_rows(target, pieces)
    side = (z_index + core) % NC
    steps = jnp.arange(NY, dtype=jnp.int32) * NC

    def plan(side):
        owner = (z_index + steps + side) % NZ // NC
        return (owner - y_index) % NY

    plan = jnp.concatenate([1 - side[None], plan(1 - side), plan(side)])
    away, *kv_own, kept = send_parts(plan, live, blocks)
    got = lax.ppermute(away, "tp", SWAP_CORE)
    after = [lax.ppermute(part, "enc", shift_x(-1)) for part in kv_own]
    before = [lax.ppermute(part, "enc", shift_x(1)) for part in kv_own]
    parts = keep_parts(live, got, kept)
    others = [lax.ppermute(parts[d], "tp", shift_y(d)) for d in FAR_LAST]
    opposite = [
        lax.ppermute(after[0], "enc", shift_x(-1)),
        lax.ppermute(before[1], "enc", shift_x(1)),
    ]
    total = parts[0].astype(F32)
    for other in others:
        total = total + other.astype(F32)
    merged = total.astype(BF)
    kv_all = [*kv_own, *after, *opposite, *before]

    moved = lax.all_to_all(merged, "enc", 0, 0, tiled=True)
    per_block = pages // (NZ * NX)
    moved = moved.reshape(NZ * NX, per_block * chunk, merged.shape[1])
    starts = lax.dynamic_slice_in_dim(page_start, enc_index * per_block, per_block)
    starts = starts - enc_index * span
    rows = (
        jnp.arange(NZ, dtype=jnp.int32)[:, None, None] * chunk
        + starts[None, :, None]
        + jnp.arange(chunk, dtype=jnp.int32)[None, None, :]
    ).reshape(1, -1)
    shifted = (y_index + jnp.arange(NY, dtype=jnp.int32)) % NY * NC
    order = jnp.concatenate([shifted - z_index, (jnp.arange(NX, dtype=jnp.int32) + x_index) % NX])
    turn = jnp.arange(2 * NY, dtype=jnp.int32) < NY
    own_heads = jnp.where(turn, (order + core) % NZ, order)
    other_heads = jnp.where(turn, (order + 1 - core) % NZ, order)
    mixed, squares = mix(rows, moved, text)
    away = project_send(other_heads, mixed, squares, kv_all)
    got = lax.ppermute(away, "tp", SWAP_CORE)
    own = project_send(own_heads, mixed, squares, kv_all)
    sums = add_pair(16, own, got)
    sums = [sums[0]] + [lax.ppermute(sums[d], "tp", shift_y(d)) for d in FAR_FIRST]

    positions = (enc_index * span + jnp.arange(span, dtype=jnp.int32)).astype(F32)
    cos, sin = rotary(positions, wide // 2)
    return tuple(finish(features * NY * NC, sums, cos, sin))


def solution(mesh):
    return jax.shard_map(
        body,
        mesh=mesh,
        in_specs=(
            P(("rep", "enc"), None, None),
            P("rep"),
            P("rep"),
            P(),
            P(),
            P(None, "tp"),
            P("tp", "enc"),
            P(("rep", "enc"), "tp"),
            P("tp"),
            P("tp", "enc"),
        ),
        out_specs=(P(("rep", "enc"), "tp"), P(("rep", "enc"), "tp")),
        check_vma=False,
    )
```
